32 devices in a mesh: expert: 8 (over z, x), tensor: 4 (over y, core).
Axes of the slice: x: 2, y: 2, z: 4, core: 2. Of those that a mesh axis runs over, the one named last changes fastest.
Arguments:
- tokens: bfloat16 [6304, 768], P('expert'), may hold values from -6 to 6
- ln1_gain: float32 [768], replicated, may hold values from 0.1 to 1.9
- ln1_bias: float32 [768], replicated, may hold values from -3 to 3
- w_qkv: bfloat16 [3, 768, 768], P(None, None, 'tensor'), may hold values from -0.21875 to 0.21875
- b_qv: float32 [2, 768], P(None, 'tensor'), may hold values from -3 to 3
- w_proj: bfloat16 [768, 768], P('tensor'), may hold values from -0.625 to 0.625
- b_proj: float32 [768], replicated, may hold values from -3 to 3
- ln2_gain: float32 [768], replicated, may hold values from 0.1 to 1.9
- ln2_bias: float32 [768], replicated, may hold values from -3 to 3
- w_router: bfloat16 [768, 8], replicated, may hold values from -0.15625 to 0.15625
- w_in: bfloat16 [8, 768, 3072], P('expert', None, 'tensor'), may hold values from -0.21875 to 0.21875
- b_in: float32 [8, 3072], P('expert', 'tensor'), may hold values from -3 to 3
- w_out: bfloat16 [8, 3072, 768], P('expert', 'tensor'), may hold values from -0.75 to 0.75
- b_out: float32 [8, 768], P('expert'), may hold values from -3 to 3
- expert_ids: int32 [6304, 2], P('expert'), may hold values from 0 to 7, all different within a row; in each aligned block of 788 rows (0 to 787, 788 to 1575, ...) at most 246 rows name the same one
- keep_mask: int32 [6304, 2], P('expert'), may hold values 0 or 1
- cotangent: float32 [6304, 768], P('expert'), may hold values from -6 to 6
Outputs:
- layer_out: float32 [6304, 768], P('expert')
- grad_tokens: float32 [6304, 768], P('expert')
- grad_ln1_gain: float32 [768], replicated
- grad_ln1_bias: float32 [768], replicated
- grad_w_qkv: float32 [3, 768, 768], P(None, None, 'tensor')
- grad_b_qv: float32 [2, 768], P(None, 'tensor')
- grad_w_proj: float32 [768, 768], P('tensor')
- grad_b_proj: float32 [768], replicated
- grad_ln2_gain: float32 [768], replicated
- grad_ln2_bias: float32 [768], replicated
- grad_w_router: float32 [768, 8], replicated
- grad_w_in: float32 [8, 768, 3072], P('expert', None, 'tensor')
- grad_b_in: float32 [8, 3072], P('expert', 'tensor')
- grad_w_out: float32 [8, 3072, 768], P('expert', 'tensor')
- grad_b_out: float32 [8, 768], P('expert')
The draws below stay inside these ranges and needn't reach their ends.
Inputs may be any that keep to these rules, and one draw needn't show every extreme that they name: `expert_ids`: each row names two different experts; among the 788 rows of one group no expert is named more than 246 times, a bound that some block reaches.
All inputs are finite; a program needn't handle non-finite values. No bound on the sum of `keep_mask` on one device may be relied on, other than what follows from the above.
Results may differ from the reference program's by a relative error of at most 0.019.
Values may be sent and summed in bfloat16 or wider, within the bound.
No kernel may reach another device: no remote copies, remote signals or barrier semaphores. Data moves between devices by JAX's collectives and lax.ppermute only.
A program may use at most 128 MiB of HBM per device.

```python
import math
import jax
import jax.numpy as jnp
import numpy as np
from jax import lax

D = 768
HEADS = 12
HEAD_DIM = 64
FF = 3072
SEQ = 197
TOK_DEV = 788
EXPERTS = 8
CAP = 246
TOKENS = 6304


def place_ends(result, own_key, least, largest):
    extent = result.shape
    place = [jax.random.randint(jax.random.fold_in(own_key, axis), (), 0, extent[axis]) for axis in range(len(extent))]
    result = result.at[tuple(place)].set(least)
    longest = extent.index(max(extent))
    place[longest] = (place[longest] + 1) % extent[longest]
    return result.at[tuple(place)].set(largest)


def block_scale(key, shape, split, low, high):
    factor_of = 1.0
    for dim, shards_of in split:
        steps = jax.random.uniform(jax.random.fold_in(jax.random.fold_in(key, 6), dim), (shards_of,), jnp.float32, low / len(split), high / len(split))
        factor_of = factor_of * jnp.repeat(jnp.exp(steps), shape[dim] // shards_of).reshape((-1,) + (1,) * (len(shape) - 1 - dim))
    return factor_of


def assign_block(own_key, own, number, rows, count, top, most, slope):
    ranking = jax.random.permutation(own_key, count)
    packed, usual = shares(count, rows * top, most, slope, True), shares(count, rows * top, most, slope, False)
    places = jnp.arange(count)

    def named(tallies, rotation):
        used = int((tallies > 0).sum())
        fixed = max(1, used // 4)
        shifted = fixed + (places - fixed + rotation * (used - fixed)) % max(1, count - fixed)
        return jnp.zeros((count,), jnp.int32).at[ranking[jnp.where(places < fixed, places, shifted)]].set(jnp.asarray(tallies, jnp.int32))

    tallies = jnp.where(number % 4 == 0, named(packed, number // 4), named(usual, number - number // 4 - 1))
    mixed = jax.random.permutation(jax.random.fold_in(own, 3), count)
    donor, taker = mixed[0:count // 2 * 2:2], mixed[1:count // 2 * 2:2]
    margin = jnp.minimum(tallies[donor] - 1, most - tallies[taker]) // 2
    margin = jnp.where((donor == ranking[0]) | (taker == ranking[0]) | (tallies[taker] == 0), 0, jnp.maximum(margin, 0))
    shifted = jax.random.randint(jax.random.fold_in(own, 4), (count // 2,), 0, 1 << 20) % (margin + 1)
    tallies = tallies.at[donor].add(-shifted).at[taker].add(shifted)
    members = jnp.searchsorted(jnp.cumsum(tallies), jnp.arange(rows * top), side="right").astype(jnp.int32)
    grid = members.reshape(top, rows).T
    grid = grid[jax.random.permutation(jax.random.fold_in(own, 1), rows)]
    rotation = jax.random.randint(jax.random.fold_in(own, 2), (rows, 1), 0, top)
    return jnp.take_along_axis(grid, (jnp.arange(top)[None, :] + rotation) % top, axis=1)


def shares(amount, total, reach, slope, full):
    loads = [(1 << 20) // math.isqrt(grade ** slope) + 1 for grade in range(1, amount + 1)]
    largest = reach if full else min(reach, max(-(-total // amount), total * loads[0] // sum(loads)))
    least = 1 if total - largest >= amount - 1 else 0
    holding, rest = [largest] + [least] * (amount - 1), total - largest - least * (amount - 1)
    while rest > 0:
        movable = [i for i in range(1, amount) if holding[i] < largest] or [i for i in range(1, amount) if holding[i] < reach]
        mass, remaining = sum([loads[i] for i in movable]), rest
        for i in movable:
            addition = min(reach - holding[i], max(1, remaining * loads[i] // mass), rest)
            holding[i] = holding[i] + addition
            rest = rest - addition
    return np.array(holding)


def normal_values(own_key, extent, scale, reach, pieces=(), held_as=jnp.bfloat16):
    gain = block_scale(own_key, extent, pieces, -0.22, 0.18) if pieces else 1.0
    entries = jax.random.normal(own_key, extent, jnp.float32) * scale * gain
    return jnp.minimum(jnp.maximum(entries, -reach), reach).astype(held_as)


def setup_inputs(seed: int = 0) -> dict:
    splits = jax.random.split(jax.random.key(seed), 18)
    tokens = normal_values(splits[0], (TOKENS, D), 1.0, 6.0, ((0, 8),))
    ln1_gain = jnp.clip(1.0 + 0.18 * jax.random.normal(splits[1], (D,), jnp.float32), 0.1, 1.9)
    ln1_bias = normal_values(splits[2], (D,), 0.3, 3.0, (), jnp.float32)
    w_qkv = normal_values(splits[3], (3, D, D), D ** -0.5, 0.21875, ((2, 4),))
    b_qv = normal_values(splits[4], (2, D), 0.3, 3.0, ((1, 4),), jnp.float32)
    w_proj = normal_values(splits[5], (D, D), (D // 8) ** -0.5, 0.625, ((0, 4),))
    b_proj = normal_values(splits[6], (D,), 0.3, 3.0, (), jnp.float32)
    ln2_gain = jnp.clip(1.0 + 0.18 * jax.random.normal(splits[7], (D,), jnp.float32), 0.1, 1.9)
    ln2_bias = normal_values(splits[8], (D,), 0.3, 3.0, (), jnp.float32)
    w_router = normal_values(splits[9], (D, EXPERTS), (2 * D) ** -0.5, 0.15625)
    w_in = normal_values(splits[10], (EXPERTS, D, FF), D ** -0.5, 0.21875, ((0, 8), (2, 4)))
    b_in = normal_values(splits[11], (EXPERTS, FF), 0.5, 3.0, ((0, 8), (1, 4)), jnp.float32)
    w_out = normal_values(splits[12], (EXPERTS, FF, D), (max(1, 3 * FF // (2 * EXPERTS * EXPERTS))) ** -0.5, 0.75, ((0, 8), (1, 4)))
    b_out = normal_values(splits[13], (EXPERTS, D), (0.05 * EXPERTS), 3.0, ((0, 8),), jnp.float32)
    expert_ids_keys = jax.random.split(jax.random.fold_in(splits[14], 1), TOKENS // TOK_DEV)
    expert_ids_turns = jax.random.permutation(jax.random.fold_in(splits[14], 3), TOKENS // TOK_DEV)
    expert_ids = jax.vmap(lambda own, number: assign_block(jax.random.fold_in(splits[14], 2), own, number, TOK_DEV, EXPERTS, 2, CAP, 1))(expert_ids_keys, expert_ids_turns).reshape((TOKENS, 2))
    keep_mask = place_ends((jax.random.randint(splits[15], (TOKENS, 2), 0, 16) < 15).astype(jnp.int32), jax.random.fold_in(splits[15], 1), 0, 1)
    cotangent = normal_values(splits[16], (TOKENS, D), 1.0, 6.0, ((0, 8),), jnp.float32)
    return {"tokens": tokens, "ln1_gain": ln1_gain, "ln1_bias": ln1_bias, "w_qkv": w_qkv, "b_qv": b_qv, "w_proj": w_proj, "b_proj": b_proj, "ln2_gain": ln2_gain, "ln2_bias": ln2_bias, "w_router": w_router, "w_in": w_in, "b_in": b_in, "w_out": w_out, "b_out": b_out, "expert_ids": expert_ids, "keep_mask": keep_mask, "cotangent": cotangent}


@jax.custom_vjp
def low(v):
    return lax.optimization_barrier(v.astype(jnp.bfloat16)).astype(jnp.float32)

@jax.custom_vjp
def low_back(v):
    return v

def low_keep(v):
    return (low(v), None)

def low_pass(kept, grad):
    return (grad,)

def back_keep(v):
    return (v, None)

def back_low(kept, grad):
    return (low(grad),)
low.defvjp(low_keep, low_pass)
low_back.defvjp(back_keep, back_low)
NORM_EPSILON = 1e-06

def norm_rows(values, gain_vec, bias_vec):
    center = values - lax.optimization_barrier(jnp.mean(values, axis=-1, keepdims=True))
    spread = lax.optimization_barrier(jnp.mean(center * center, axis=-1, keepdims=True))
    return center * lax.rsqrt(spread + NORM_EPSILON) * gain_vec + bias_vec

def exact_gelu(values):
    return jax.nn.gelu(values, approximate=False)

def low_both(values):
    return low(low_back(values))

def reference(tokens, ln1_gain, ln1_bias, w_qkv, b_qv, w_proj, b_proj, ln2_gain, ln2_bias, w_router, w_in, b_in, w_out, b_out, expert_ids, keep_mask, cotangent):
    groups = TOKENS // TOK_DEV
    rows_all = EXPERTS * groups * CAP
    labels = jnp.arange(EXPERTS, dtype=jnp.int32)
    member = ((expert_ids[:, :, None] == labels[None, None, :]) & (keep_mask[:, :, None] > 0)).astype(jnp.int32)
    member = member.reshape(groups, TOK_DEV * 2, EXPERTS)
    before = jnp.cumsum(member, axis=1) - member
    slot_index = lax.optimization_barrier(jnp.sum(before * member, axis=2)).reshape(TOKENS, 2)
    group_index = (jnp.arange(TOKENS, dtype=jnp.int32) // TOK_DEV)[:, None]
    target = expert_ids * (groups * CAP) + group_index * CAP + slot_index
    target = jnp.where(keep_mask > 0, target, rows_all).astype(jnp.int32).reshape(TOKENS * 2)
    kept_mask = (keep_mask > 0).astype(jnp.float32)
    factor = HEAD_DIM ** (-0.5)
    images = TOKENS // SEQ
    highest = lax.Precision.HIGHEST

    def layer(inputs, gain_one, bias_one, w_triple, b_pair, w_mix, b_mix, gain_two, bias_two, w_route, w_first, b_first, w_second, b_second):
        normed = low(norm_rows(inputs, gain_one, bias_one))
        queries = low_both(jnp.dot(normed, w_triple[0], precision=highest) + b_pair[0]).reshape(images, SEQ, HEADS, HEAD_DIM)
        keys_all = low_both(jnp.dot(normed, w_triple[1], precision=highest)).reshape(images, SEQ, HEADS, HEAD_DIM)
        values_all = low_both(jnp.dot(normed, w_triple[2], precision=highest) + b_pair[1]).reshape(images, SEQ, HEADS, HEAD_DIM)
        scores = low_back(jnp.einsum('iqhd,ikhd->ihqk', queries, keys_all, precision=highest) * factor)
        weights = low(jax.nn.softmax(scores, axis=-1))
        mixed = low_both(jnp.einsum('ihqk,ikhd->iqhd', weights, values_all, precision=highest).reshape(TOKENS, D))
        residual = inputs + low_back(jnp.dot(mixed, w_mix, precision=highest) + b_mix)
        routed = low(norm_rows(residual, gain_two, bias_two))
        route_probs = jax.nn.softmax(low_back(jnp.dot(routed, w_route, precision=highest)), axis=-1)
        gates_kept = jnp.take_along_axis(route_probs, expert_ids, axis=1) * kept_mask
        spread_rows = (routed[:, None, :] * kept_mask[:, :, None]).reshape(TOKENS * 2, D)
        buffer = jnp.zeros((rows_all + 1, D), jnp.float32).at[target].add(spread_rows)
        buffer = low_back(buffer[:rows_all].reshape(EXPERTS, groups * CAP, D))
        pre_act = low_back(jnp.einsum('erd,edf->erf', buffer, w_first, precision=highest) + b_first[:, None, :])
        hidden = low(exact_gelu(pre_act))
        expert_rows = low_both(jnp.einsum('erf,efd->erd', hidden, w_second, precision=highest) + b_second[:, None, :])
        padded = jnp.concatenate([expert_rows.reshape(rows_all, D), jnp.zeros((1, D), jnp.float32)], axis=0)
        picked = padded[target].reshape(TOKENS, 2, D)
        return residual + lax.optimization_barrier(jnp.sum(gates_kept[:, :, None] * picked, axis=1))
    layer_out, back_fn = jax.vjp(layer, tokens.astype(jnp.float32), ln1_gain.astype(jnp.float32), ln1_bias.astype(jnp.float32), w_qkv.astype(jnp.float32), b_qv.astype(jnp.float32), w_proj.astype(jnp.float32), b_proj.astype(jnp.float32), ln2_gain.astype(jnp.float32), ln2_bias.astype(jnp.float32), w_router.astype(jnp.float32), w_in.astype(jnp.float32), b_in.astype(jnp.float32), w_out.astype(jnp.float32), b_out.astype(jnp.float32))
    grads = back_fn(cotangent.astype(jnp.float32))
    return (layer_out, grads[0], grads[1], grads[2], grads[3], grads[4], grads[5], grads[6], grads[7], grads[8], grads[9], grads[10], grads[11], grads[12], grads[13])
```

```python
import jax
import jax.numpy as jnp
from jax import lax
from jax.experimental import pallas as pl
from jax.experimental.pallas import tpu as pltpu
from jax.sharding import PartitionSpec as P

HEAD_DIM = 64
SEQ = 197
NORM_EPSILON = 1e-06
LOW = jnp.bfloat16
WIDE = jnp.float32
ROOT_HALF = 0.7071067811865476
DENSITY = 0.3989422804014327


def norm_parts(values):
    center = values - jnp.mean(values, axis=-1, keepdims=True)
    spread = jnp.mean(center * center, axis=-1, keepdims=True)
    scale = lax.rsqrt(spread + NORM_EPSILON)
    return center * scale, scale


def norm_back(unit, scale, gain_vec, grad):
    grad_unit = grad * gain_vec
    first = jnp.mean(grad_unit, axis=-1, keepdims=True)
    second = jnp.mean(grad_unit * unit, axis=-1, keepdims=True)
    return scale * (grad_unit - first - unit * second)


def dot_wide(equation, left, right):
    return jnp.einsum(equation, left, right, preferred_element_type=WIDE)


def swap(value, step):
    size = lax.axis_size("tensor")
    return lax.ppermute(value, "tensor", [(i, i ^ step) for i in range(size)])


def tensor_order():
    order, step = [0], lax.axis_size("tensor") // 2
    while step:
        order, step = order + [i ^ step for i in order], step // 2
    return order


def gather_list(block):
    blocks, step = [block], lax.axis_size("tensor") // 2
    while step:
        blocks, step = blocks + [swap(b, step) for b in blocks], step // 2
    return blocks


def scatter_sum(blocks):
    step = 1
    while len(blocks) > 1:
        half = len(blocks) // 2
        arrived = [swap(b.astype(LOW), step) for b in blocks[half:]]
        blocks = [b + a.astype(WIDE) for b, a in zip(blocks[:half], arrived)]
        step *= 2
    return blocks[0]


def tensor_sum(value):
    step = 1
    while step < lax.axis_size("tensor"):
        value, step = value + swap(value, step), step * 2
    return value


def placed_blocks(blocks, axis):
    me, extent = lax.axis_index("tensor"), blocks[0].shape[axis]
    shape = list(blocks[0].shape)
    shape[axis] = extent * len(blocks)
    result = jnp.zeros(shape, blocks[0].dtype)
    for o, block in zip(tensor_order(), blocks):
        result = lax.dynamic_update_slice_in_dim(result, block, (me ^ o) * extent, axis)
    return result


def exchange(rows):
    return lax.all_to_all(rows, "expert", 0, 0, tiled=True)


def shift(value, step):
    size = lax.axis_size("expert")
    return lax.ppermute(value, "expert", [(i, (i + step) % size) for i in range(size)])


def expert_sum(parts, *beside):
    size, me = lax.axis_size("expert"), lax.axis_index("expert")
    if size > 8:
        return lax.psum(parts, "expert"), *beside
    low = parts.astype(LOW)
    mine = lax.dynamic_index_in_dim(parts, me, 0, keepdims=False)
    moved = [
        shift(lax.dynamic_index_in_dim(low, (me + step) % size, 0, keepdims=False), step)
        for step in range(1, size)
    ]
    total = (mine + sum(part.astype(WIDE) for part in moved)).astype(LOW)
    total, *beside = together(total, *beside)
    blocks, order, step = total[None], [0], size // 2
    while step:
        pairs = [(i, i ^ step) for i in range(size)]
        blocks = jnp.concatenate([blocks, lax.ppermute(blocks, "expert", pairs)], axis=0)
        order, step = order + [i ^ step for i in order], step // 2
    result = jnp.zeros(parts.shape, LOW)
    for place, o in enumerate(order):
        result = lax.dynamic_update_index_in_dim(result, blocks[place], me ^ o, 0)
    return result.astype(WIDE), *beside


def halves(value):
    high = lax.reduce_precision(value, 8, 7)
    return high, value - high


def together(*values):
    return lax.optimization_barrier(values)


def dims(left, right):
    return (((left,), (right,)), ((), ()))


def low_dot(left, right, contract):
    return lax.dot_general(
        left.astype(LOW), right.astype(LOW), contract, preferred_element_type=WIDE
    )


def softmax_rows(queries, keys):
    scores = low_dot(queries, keys, dims(1, 1)) * HEAD_DIM ** (-0.5)
    powers = jnp.exp(scores - jnp.max(scores, axis=-1, keepdims=True))
    return powers / jnp.sum(powers, axis=-1, keepdims=True)


def attend_kernel(tok_ref, gain_ref, bias_ref, w_ref, b_ref, normed_ref, triple_ref, mixed_ref, hold):
    unit, _ = norm_parts(tok_ref[...].astype(WIDE))
    normed = (unit * gain_ref[...] + bias_ref[...]).astype(LOW)
    normed_ref[...] = normed
    cols = w_ref.shape[2]
    for j in range(3):
        part = jnp.dot(normed, w_ref[j], preferred_element_type=WIDE)
        if j != 1:
            part = part + b_ref[j // 2 : j // 2 + 1, :]
        part = part.astype(LOW)
        triple_ref[j] = part
        hold[j] = part.astype(WIDE)
    for i in range(tok_ref.shape[0] // SEQ):
        rows = pl.ds(i * SEQ, SEQ)
        queries, keys, values = hold[0, rows, :], hold[1, rows, :], hold[2, rows, :]
        parts = []
        for at in range(0, cols, HEAD_DIM):
            head = slice(at, at + HEAD_DIM)
            probs = softmax_rows(queries[:, head], keys[:, head])
            parts.append(low_dot(probs, values[:, head], dims(1, 0)))
        hold[0, rows, :] = jnp.concatenate(parts, axis=1)
    mixed_ref[...] = hold[0].T.astype(LOW)


def attend(tokens, gain, bias, w_qkv, b_qv):
    count, width = tokens.shape
    cols = w_qkv.shape[2]
    return pl.pallas_call(
        attend_kernel,
        out_shape=(
            jax.ShapeDtypeStruct((count, width), LOW),
            jax.ShapeDtypeStruct((3, count, cols), LOW),
            jax.ShapeDtypeStruct((cols, count), LOW),
        ),
        scratch_shapes=[pltpu.VMEM((3, count, cols), WIDE)],
        compiler_params=pltpu.CompilerParams(vmem_limit_bytes=40 * 2**20),
        name="attend",
    )(tokens, gain[None], bias[None], w_qkv, b_qv)


def attend_back_kernel(grad_ref, w_ref, triple_ref, out_ref, hold, grad_hold):
    cols = w_ref.shape[0]
    grad = lax.dot_general(grad_ref[...], w_ref[...], dims(1, 1), preferred_element_type=WIDE)
    grad_hold[...] = grad.astype(LOW).astype(WIDE)
    for j in range(3):
        hold[j] = triple_ref[j].astype(WIDE)
    factor = HEAD_DIM ** (-0.5)
    for i in range(grad_ref.shape[0] // SEQ):
        rows = pl.ds(i * SEQ, SEQ)
        queries, keys, values = hold[0, rows, :], hold[1, rows, :], hold[2, rows, :]
        grads = grad_hold[rows, :]
        parts = [[], [], []]
        for at in range(0, cols, HEAD_DIM):
            head = slice(at, at + HEAD_DIM)
            q, k, v, g = queries[:, head], keys[:, head], values[:, head], grads[:, head]
            probs = softmax_rows(q, k)
            d_probs = low_dot(g, v, dims(1, 1))
            d_scores = probs * (d_probs - jnp.sum(probs * d_probs, axis=-1, keepdims=True))
            parts[0].append(low_dot(d_scores, k, dims(1, 0)) * factor)
            parts[1].append(low_dot(d_scores, q, dims(0, 0)) * factor)
            parts[2].append(low_dot(probs, g, dims(0, 0)))
        for j in range(3):
            hold[j, rows, :] = jnp.concatenate(parts[j], axis=1)
    for j in range(3):
        out_ref[j] = hold[j].astype(LOW)


def attend_back(d_attn, w_proj, triple):
    _, count, cols = triple.shape
    return pl.pallas_call(
        attend_back_kernel,
        out_shape=jax.ShapeDtypeStruct(triple.shape, LOW),
        scratch_shapes=[pltpu.VMEM((3, count, cols), WIDE), pltpu.VMEM((count, cols), WIDE)],
        compiler_params=pltpu.CompilerParams(vmem_limit_bytes=40 * 2**20),
        name="attend_back",
    )(d_attn, w_proj, triple)


def on_device(
    tokens,
    ln1_gain,
    ln1_bias,
    w_qkv,
    b_qv,
    w_proj,
    b_proj,
    ln2_gain,
    ln2_bias,
    w_router,
    w_in,
    b_in,
    w_out,
    b_out,
    expert_ids,
    keep_mask,
    cotangent,
):
    tok_count, width = tokens.shape
    experts = w_router.shape[1]
    capacity = max(2, (2 * tok_count + experts - 1) // experts * 5 // 4)
    ranks = lax.axis_size("tensor")
    me_t, me_e = lax.axis_index("tensor"), lax.axis_index("expert")
    share = -(-capacity // (8 * ranks)) * 8
    local_cols = w_qkv.shape[2]
    order = tensor_order()

    far = ranks // 2
    cuts = (0, width // 4 * 3, width)
    w_in_cuts = [swap(w_in[0, a:b], far) for a, b in zip(cuts[:-1], cuts[1:])]
    w_out_all = [w_out[0], swap(w_out[0], far)]
    b_in_all = [b_in[0], swap(b_in[0], far)]
    proj_all = placed_blocks(gather_list(w_proj), 0)

    ids = expert_ids.T
    kept = keep_mask.T > 0
    labels = jnp.arange(experts, dtype=jnp.int32)
    chosen = (ids[:, None, :] == labels[None, :, None])
    member = jnp.sum((chosen & kept[:, None, :]).astype(WIDE), axis=0)
    places = jnp.arange(tok_count, dtype=jnp.int32)
    earlier = (places[:, None] < places[None, :]).astype(LOW)
    before = dot_wide("et,ts->es", member.astype(LOW), earlier)
    slot = jnp.sum(jnp.where(chosen, before[None], 0.0), axis=1).astype(jnp.int32)
    holder = slot // share
    inner = ids * share + slot % share
    own_rows = experts * share
    own_place = jnp.where(kept & (holder == me_t), inner, -1)
    row_labels = jnp.arange(own_rows, dtype=jnp.int32)[:, None]
    own_hot = ((row_labels == own_place[0:1]) | (row_labels == own_place[1:2])).astype(LOW)
    all_place = jnp.where(kept, holder * own_rows + inner, -1)
    all_labels = jnp.arange(ranks * own_rows, dtype=jnp.int32)[:, None]
    all_hot = ((all_labels == all_place[0:1]) | (all_labels == all_place[1:2])).astype(LOW)

    inputs = tokens.astype(WIDE)
    unit_one, scale_one = norm_parts(inputs)
    cot_rows = dot_wide("rt,td->rd", own_hot, cotangent.astype(LOW)).astype(LOW)
    own_tokens, cot_rows = together(tokens, cot_rows)
    cot_here = exchange(cot_rows)
    normed_low, triple, mixed_low = attend(own_tokens, ln1_gain, ln1_bias, w_qkv, b_qv)
    mixed_low, w_in_cuts[0] = together(mixed_low, w_in_cuts[0])
    mixed_all = placed_blocks(gather_list(mixed_low), 0)
    residual = inputs + (dot_wide("ct,cd->td", mixed_all, proj_all) + b_proj)
    unit_two, scale_two = norm_parts(residual)
    routed_low = (unit_two * ln2_gain + ln2_bias).astype(LOW)

    sent_rows = dot_wide("rt,td->rd", own_hot, routed_low).astype(LOW)
    sent_rows, cot_here, w_in_cuts[1] = together(sent_rows, cot_here, w_in_cuts[1])
    rows_here = exchange(sent_rows)
    rows_here, w_out_far = together(rows_here, w_out_all[1])
    w_out_all = [w_out_all[0], w_out_far]
    w_in_all = [w_in[0], jnp.concatenate(w_in_cuts, axis=0)]
    rows_here = jnp.concatenate([rows_here, swap(rows_here, 1)], axis=0)
    cot_here = jnp.concatenate([cot_here, swap(cot_here, 1)], axis=0)

    row_route = jax.nn.softmax(dot_wide("de,rd->er", w_router, rows_here), axis=0)
    row_gate = lax.dynamic_index_in_dim(row_route, me_e, 0, keepdims=False)
    pre_acts = [dot_wide("rd,df->rf", rows_here, w) + b for w, b in zip(w_in_all, b_in_all)]
    below = [0.5 * (1.0 + lax.erf(v * ROOT_HALF)) for v in pre_acts]
    hidden = [(v * c).astype(LOW) for v, c in zip(pre_acts, below)]
    slopes = [
        (c + v * (DENSITY * jnp.exp(-0.5 * v * v))).astype(LOW) for v, c in zip(pre_acts, below)
    ]
    out_part = dot_wide("rf,fd->rd", hidden[0], w_out_all[0])
    out_part = out_part + dot_wide("rf,fd->rd", hidden[1], w_out_all[1])
    d_rows = (row_gate[:, None] * cot_here.astype(WIDE)).astype(LOW)
    d_pre = [
        (dot_wide("rd,fd->rf", d_rows, w) * s.astype(WIDE)).astype(LOW)
        for w, s in zip(w_out_all, slopes)
    ]
    back_part = dot_wide("rf,df->rd", d_pre[0], w_in_all[0])
    back_part = back_part + dot_wide("rf,df->rd", d_pre[1], w_in_all[1])
    swapped = jnp.concatenate([out_part[own_rows:], back_part[own_rows:]], axis=0)
    swapped = swap(swapped.astype(LOW), 1).astype(WIDE)
    out_rows = (out_part[:own_rows] + swapped[:own_rows] + b_out[0]).astype(LOW)
    back_rows = (back_part[:own_rows] + swapped[own_rows:]).astype(LOW)
    home = [r.reshape(experts, share, width) for r in (out_rows, back_rows)]
    home = exchange(jnp.concatenate(home, axis=1))

    far_out = dot_wide("rf,rd->fd", hidden[1], d_rows).astype(LOW)
    far_in = dot_wide("rd,rf->df", rows_here, d_pre[1]).astype(LOW)
    out_arrived = swap(far_out, far)
    near_out = dot_wide("rf,rd->fd", hidden[0], d_rows)
    near_in = dot_wide("rd,rf->df", rows_here, d_pre[0])
    sums_out = jnp.sum(jnp.sum(d_rows.astype(WIDE).reshape(2, own_rows, width), axis=1), axis=0)
    sums_in = [jnp.sum(d.astype(WIDE), axis=0) for d in d_pre]
    grad_b_in = sums_in[0] + swap(sums_in[1], far)
    grad_b_out = sums_out + swap(sums_out, far)

    route = jax.nn.softmax(dot_wide("de,td->et", w_router, routed_low), axis=0)
    hot_blocks = own_hot.reshape(experts, share, tok_count).astype(WIDE)
    slot_gate = jnp.sum(hot_blocks * route[:, None, :], axis=2).reshape(own_rows, 1)
    home, out_arrived = together(home, out_arrived)
    grad_w_out = near_out + out_arrived.astype(WIDE)
    out_home = home[:, :share].reshape(own_rows, width)
    back_home = home[:, share:].reshape(own_rows, width)
    slot_grad = jnp.sum(cot_rows.astype(WIDE) * out_home.astype(WIDE), axis=1)
    extra = -(-2 * own_rows // (16 * width)) * 16
    both = jnp.stack(halves(slot_grad)).reshape(-1)
    both = jnp.pad(both, (0, extra * width - 2 * own_rows)).astype(LOW).reshape(extra, width)
    gathered = gather_list(jnp.concatenate([back_home, both], axis=0))
    back_all = placed_blocks([g[:own_rows] for g in gathered], 0)
    both = [g[own_rows:].reshape(-1)[: 2 * own_rows].reshape(2, own_rows) for g in gathered]
    both = placed_blocks(both, 1).reshape(2, 1, ranks, experts, share)
    mask = (labels[:, None] == labels[None, :]).astype(LOW)
    both = (both * mask[None, :, None, :, None]).reshape(2 * experts, ranks * own_rows)
    d_route = jnp.sum(dot_wide("er,rt->et", both, all_hot).reshape(2, experts, -1), axis=0)
    d_logits = (route * (d_route - jnp.sum(d_route * route, axis=0, keepdims=True))).astype(LOW)
    grad_router = dot_wide("et,td->ed", d_logits, routed_low)
    gated = (slot_gate * out_home.astype(WIDE)).astype(LOW)
    back_all, gated, grad_w_out = together(back_all, gated, grad_w_out)
    gated_all = placed_blocks(gather_list(gated), 0)
    d_routed = dot_wide("et,de->td", d_logits, w_router)
    d_routed = d_routed + dot_wide("rt,rd->td", all_hot, back_all)
    grad_ln2_gain = jnp.sum(d_routed * unit_two, axis=0)
    grad_ln2_bias = jnp.sum(d_routed, axis=0)
    d_residual = cotangent + norm_back(unit_two, scale_two, ln2_gain, d_routed)
    d_attn = d_residual.astype(LOW)
    d_attn, far_in, gated_all = together(d_attn, far_in, gated_all)
    layer_out = residual + dot_wide("rt,rd->td", all_hot, gated_all)
    in_arrived = swap(far_in, far)
    grad_b_proj = jnp.sum(d_attn.astype(WIDE), axis=0)
    grad_w_proj = dot_wide("ct,td->cd", mixed_low, d_attn)

    d_triple = attend_back(d_attn, w_proj, triple)
    grad_w_qkv = dot_wide("jtc,td->jcd", d_triple, normed_low)
    grad_b_qv = jnp.stack(
        [jnp.sum(d_triple[0].astype(WIDE), axis=0), jnp.sum(d_triple[2].astype(WIDE), axis=0)]
    )
    d_normed_part = dot_wide("jtc,jdc->td", d_triple, w_qkv)
    grad_ln1_gain = jnp.sum(d_normed_part * unit_one, axis=0)
    grad_ln1_bias = jnp.sum(d_normed_part, axis=0)

    groups = lax.axis_size("expert")
    pair = jnp.pad(grad_b_qv.reshape(1, -1), ((0, 0), (0, width - 2 * local_cols)))
    small = jnp.stack(
        [grad_ln1_gain, grad_ln1_bias, grad_ln2_gain, grad_ln2_bias, grad_b_proj]
    )
    small = jnp.concatenate([small, pair, grad_router], axis=0)
    count = small.shape[0]
    each = -(-count // groups)
    small = jnp.pad(small, ((0, groups * each - count), (0, 0))).reshape(groups, each, width)
    high, rest = halves(small)
    parts = grad_w_qkv.reshape(groups, -1, width)
    body = parts.shape[1]
    proj_parts = grad_w_proj.reshape(groups, -1, width)
    tail = body + 2 * each
    parts = jnp.concatenate([parts, high, rest, proj_parts], axis=1)
    proj_rows = proj_parts.shape[1]
    parts = jnp.pad(parts, ((0, 0), (0, -parts.shape[1] % 8), (0, 0)))
    parts, d_normed_part = expert_sum(parts, d_normed_part)

    rows_each = -(-tok_count // (8 * ranks)) * 8
    fill = ranks * rows_each - tok_count

    def rows_of(value, index):
        padded = jnp.pad(value, ((0, fill), (0, 0)))
        return lax.dynamic_slice_in_dim(padded, index * rows_each, rows_each, 0)

    d_normed = scatter_sum([rows_of(d_normed_part, me_t ^ o) for o in order])
    d_normed, in_arrived = together(d_normed, in_arrived)
    grad_w_in = near_in + in_arrived.astype(WIDE)
    d_share = norm_back(rows_of(unit_one, me_t), rows_of(scale_one, me_t), ln1_gain, d_normed)
    d_inputs = placed_blocks(gather_list(d_share.astype(LOW)), 0)[:tok_count]
    grad_tokens = d_residual + d_inputs.astype(WIDE)

    proj_sum = parts[:, tail : tail + proj_rows].reshape(local_cols, width)
    qkv_sum = jnp.swapaxes(parts[:, :body].reshape(3, local_cols, width), 1, 2)
    small = parts[:, body : body + each] + parts[:, body + each : body + 2 * each]
    small = small.reshape(groups * each, width)
    norm_sum = tensor_sum(small[:2])
    return (
        layer_out,
        grad_tokens,
        norm_sum[0],
        norm_sum[1],
        qkv_sum,
        small[5, : 2 * local_cols].reshape(2, local_cols),
        proj_sum,
        small[4],
        small[2],
        small[3],
        small[6 : 6 + experts].T,
        grad_w_in[None],
        grad_b_in[None],
        grad_w_out[None],
        grad_b_out[None],
    )


def solution(mesh):
    placed = (
        P("expert", None),
        P(),
        P(),
        P(None, None, "tensor"),
        P(None, "tensor"),
        P("tensor", None),
        P(),
        P(),
        P(),
        P(),
        P("expert", None, "tensor"),
        P("expert", "tensor"),
        P("expert", "tensor", None),
        P("expert", None),
        P("expert", None),
        P("expert", None),
        P("expert", None),
    )
    return jax.shard_map(
        on_device,
        mesh=mesh,
        in_specs=placed,
        out_specs=(
            P("expert", None),
            P("expert", None),
            P(),
            P(),
            P(None, None, "tensor"),
            P(None, "tensor"),
            P("tensor", None),
            P(),
            P(),
            P(),
            P(),
            P("expert", None, "tensor"),
            P("expert", "tensor"),
            P("expert", "tensor", None),
            P("expert", None),
        ),
        check_vma=False,
    )
```

```python
import functools

import jax
import jax.numpy as jnp
from jax import lax
from jax.experimental import pallas as pl
from jax.experimental.pallas import tpu as pltpu
from jax.sharding import PartitionSpec as P

HEAD_DIM = 64
SEQ = 197
NORM_EPSILON = 1e-06
LOW = jnp.bfloat16
WIDE = jnp.float32
ROOT_HALF = 0.7071067811865476
DENSITY = 0.3989422804014327


def norm_parts(values):
    center = values - jnp.mean(values, axis=-1, keepdims=True)
    spread = jnp.mean(center * center, axis=-1, keepdims=True)
    scale = lax.rsqrt(spread + NORM_EPSILON)
    return center * scale, scale


def norm_back(unit, scale, gain_vec, grad):
    grad_unit = grad * gain_vec
    first = jnp.mean(grad_unit, axis=-1, keepdims=True)
    second = jnp.mean(grad_unit * unit, axis=-1, keepdims=True)
    return scale * (grad_unit - first - unit * second)


def dot_wide(equation, left, right):
    return jnp.einsum(equation, left, right, preferred_element_type=WIDE)


def swap(value, step):
    size = lax.axis_size("tensor")
    return lax.ppermute(value, "tensor", [(i, i ^ step) for i in range(size)])


def tensor_order():
    order, step = [0], lax.axis_size("tensor") // 2
    while step:
        order, step = order + [i ^ step for i in order], step // 2
    return order


def gather_list(block, far_block=None):
    blocks, step = [block], lax.axis_size("tensor") // 2
    if far_block is not None:
        blocks, step = [block, far_block], step // 2
    while step:
        blocks, step = blocks + [swap(b, step) for b in blocks], step // 2
    return blocks


def placed_blocks(blocks, axis):
    me, extent = lax.axis_index("tensor"), blocks[0].shape[axis]
    shape = list(blocks[0].shape)
    shape[axis] = extent * len(blocks)
    result = jnp.zeros(shape, blocks[0].dtype)
    for o, block in zip(tensor_order(), blocks):
        result = lax.dynamic_update_slice_in_dim(result, block, (me ^ o) * extent, axis)
    return result


def exchange(rows):
    return lax.all_to_all(rows, "expert", 0, 0, tiled=True)


def shift(value, step):
    size = lax.axis_size("expert")
    return lax.ppermute(value, "expert", [(i, (i + step) % size) for i in range(size)])


def unpack_kernel(body, proj, each, me_ref, *refs):
    size = len(refs) - 3
    proj_ref, qkv_ref, small_ref = refs[size:]
    for step in range(size):
        at = lax.rem(me_ref[0] + size - step, size)
        block = refs[step][...].astype(WIDE)
        qkv_ref[pl.ds(pl.multiple_of(at * body, 8), body), :] = block[:body]
        proj_ref[pl.ds(pl.multiple_of(at * proj, 8), proj), :] = block[body : body + proj]
        end = body + proj
        small_ref[at] = block[end : end + each] + block[end + each : end + 2 * each]


def expert_sum(parts, body, proj, each, beside):
    size, me = lax.axis_size("expert"), lax.axis_index("expert")
    width, end = parts.shape[2], body + proj
    if size > 8:
        total = lax.psum(parts, "expert")
        small = total[:, end : end + each] + total[:, end + each : end + 2 * each]
        return total[:, body:end], total[:, :body], small, beside(small)
    low = parts.astype(LOW)
    mine = lax.dynamic_index_in_dim(parts, me, 0, keepdims=False)
    moved = [
        shift(lax.dynamic_index_in_dim(low, (me + step) % size, 0, keepdims=False), step)
        for step in range(1, size)
    ]
    total = (mine + sum(part.astype(WIDE) for part in moved)).astype(LOW)
    blocks = [total] + [shift(total, step) for step in range(1, size)]
    others = beside(blocks[1])
    whole = pl.BlockSpec(memory_space=pltpu.VMEM)
    results = pl.pallas_call(
        functools.partial(unpack_kernel, body, proj, each),
        out_shape=(
            jax.ShapeDtypeStruct((size * proj, width), WIDE),
            jax.ShapeDtypeStruct((size * body, width), WIDE),
            jax.ShapeDtypeStruct((size, each, width), WIDE),
        ),
        in_specs=[pl.BlockSpec(memory_space=pltpu.SMEM)] + [whole] * size,
        out_specs=[whole] * 3,
        compiler_params=pltpu.CompilerParams(vmem_limit_bytes=40 * 2**20),
        name="unpack",
    )(me.astype(jnp.int32).reshape(1), *blocks)
    return *results, others


def halves(value):
    high = lax.reduce_precision(value, 8, 7)
    return high, value - high


def together(*values):
    return lax.optimization_barrier(values)


def dims(left, right):
    return (((left,), (right,)), ((), ()))


def low_dot(left, right, contract):
    return lax.dot_general(
        left.astype(LOW), right.astype(LOW), contract, preferred_element_type=WIDE
    )


def softmax_rows(queries, keys):
    scores = low_dot(queries, keys, dims(1, 1)) * HEAD_DIM ** (-0.5)
    powers = jnp.exp(scores - jnp.max(scores, axis=-1, keepdims=True))
    return powers / jnp.sum(powers, axis=-1, keepdims=True)


def attend_kernel(tok_ref, gain_ref, bias_ref, w_ref, b_ref, normed_ref, triple_ref, mixed_ref, hold):
    unit, _ = norm_parts(tok_ref[...].astype(WIDE))
    normed = (unit * gain_ref[...] + bias_ref[...]).astype(LOW)
    normed_ref[...] = normed
    cols = w_ref.shape[2]
    for j in range(3):
        part = jnp.dot(normed, w_ref[j], preferred_element_type=WIDE)
        if j != 1:
            part = part + b_ref[j // 2 : j // 2 + 1, :]
        part = part.astype(LOW)
        triple_ref[j] = part
        hold[j] = part.astype(WIDE)
    for i in range(tok_ref.shape[0] // SEQ):
        rows = pl.ds(i * SEQ, SEQ)
        queries, keys, values = hold[0, rows, :], hold[1, rows, :], hold[2, rows, :]
        parts = []
        for at in range(0, cols, HEAD_DIM):
            head = slice(at, at + HEAD_DIM)
            probs = softmax_rows(queries[:, head], keys[:, head])
            parts.append(low_dot(probs, values[:, head], dims(1, 0)))
        hold[0, rows, :] = jnp.concatenate(parts, axis=1)
    mixed_ref[...] = hold[0].T.astype(LOW)


def attend(tokens, gain, bias, w_qkv, b_qv):
    count, width = tokens.shape
    cols = w_qkv.shape[2]
    return pl.pallas_call(
        attend_kernel,
        out_shape=(
            jax.ShapeDtypeStruct((count, width), LOW),
            jax.ShapeDtypeStruct((3, count, cols), LOW),
            jax.ShapeDtypeStruct((cols, count), LOW),
        ),
        scratch_shapes=[pltpu.VMEM((3, count, cols), WIDE)],
        compiler_params=pltpu.CompilerParams(vmem_limit_bytes=40 * 2**20),
        name="attend",
    )(tokens, gain[None], bias[None], w_qkv, b_qv)


def attend_back(queries, keys, values, grads):
    factor = HEAD_DIM ** (-0.5)
    parts = [[], [], []]
    for at in range(0, queries.shape[1], HEAD_DIM):
        head = slice(at, at + HEAD_DIM)
        q, k, v, g = queries[:, head], keys[:, head], values[:, head], grads[:, head]
        probs = softmax_rows(q, k)
        d_probs = low_dot(g, v, dims(1, 1))
        d_scores = probs * (d_probs - jnp.sum(probs * d_probs, axis=-1, keepdims=True))
        parts[0].append(low_dot(d_scores, k, dims(1, 0)) * factor)
        parts[1].append(low_dot(d_scores, q, dims(0, 0)) * factor)
        parts[2].append(low_dot(probs, g, dims(0, 0)))
    return [jnp.concatenate(p, axis=1) for p in parts]


def home_kernel(order, own_rows, share, me_ref, *refs):
    ranks = len(order)
    blocks, marks, refs = refs[:ranks], refs[ranks : 2 * ranks], refs[2 * ranks :]
    hot_ref, route_ref, router_ref, res_ref, cot_ref, gain_ref, proj_ref, triple_ref = refs[:8]
    d_res_ref, d_attn_ref, d_triple_ref, d_logits_ref, sums_ref, hold, total = refs[8:]
    experts = route_ref.shape[0]
    spread = 0.0
    line = lax.broadcasted_iota(jnp.int32, (2 * experts, own_rows), 0) % experts
    mask = line == lax.broadcasted_iota(jnp.int32, (2 * experts, own_rows), 1) // share
    for p, o in enumerate(order):
        start = pl.multiple_of((me_ref[0] ^ o) * own_rows, own_rows)
        hot = hot_ref[:, pl.ds(start, own_rows)]
        part = jnp.dot(hot, blocks[p][...], preferred_element_type=WIDE)
        total[...] = part if p == 0 else total[...] + part
        mark = marks[p][...].astype(WIDE)[:, :share]
        mark = jnp.where(mask, jnp.concatenate([mark] * experts, axis=1), 0.0)
        spread = spread + low_dot(mark, hot, dims(1, 1))
    d_route = spread[:experts] + spread[experts:]
    route = route_ref[...]
    inner = jnp.sum(d_route * route, axis=0, keepdims=True)
    d_logits = (route * (d_route - inner)).astype(LOW)
    d_logits_ref[...] = d_logits
    total[...] += low_dot(d_logits, router_ref[...], dims(0, 0))
    for j in range(3):
        hold[j] = triple_ref[j].astype(WIDE)
    sums = [0.0, 0.0, 0.0]
    for i in range(res_ref.shape[0] // SEQ):
        rows = pl.ds(i * SEQ, SEQ)
        d_routed = total[rows, :]
        unit, scale = norm_parts(res_ref[rows, :])
        d_residual = cot_ref[rows, :] + norm_back(unit, scale, gain_ref[...], d_routed)
        d_res_ref[rows, :] = d_residual
        d_attn = d_residual.astype(LOW)
        wide = d_attn.astype(WIDE)
        total[rows, :] = wide
        for n, term in enumerate((d_routed * unit, d_routed, wide)):
            sums[n] = sums[n] + jnp.sum(term, axis=0, keepdims=True)
        d_mixed = lax.dot_general(d_attn, proj_ref[...], dims(1, 1), preferred_element_type=WIDE)
        d_mixed = d_mixed.astype(LOW).astype(WIDE)
        parts = attend_back(hold[0, rows, :], hold[1, rows, :], hold[2, rows, :], d_mixed)
        for j in range(3):
            hold[j, rows, :] = parts[j]
    d_attn_ref[...] = total[...].astype(LOW)
    for j in range(3):
        d_triple_ref[j] = hold[j].astype(LOW)
    sums_ref[...] = jnp.concatenate(sums, axis=0)


def home(order, own_rows, share, me, blocks, marks, hot, route, router, res, cot, gain, proj, triple):
    _, count, cols = triple.shape
    width = res.shape[1]
    kernel = functools.partial(home_kernel, order, own_rows, share)
    whole = pl.BlockSpec(memory_space=pltpu.VMEM)
    operands = (*blocks, *marks, hot, route, router, res, cot, gain[None], proj, triple)
    return pl.pallas_call(
        kernel,
        out_shape=(
            jax.ShapeDtypeStruct((count, width), WIDE),
            jax.ShapeDtypeStruct((count, width), LOW),
            jax.ShapeDtypeStruct(triple.shape, LOW),
            jax.ShapeDtypeStruct(route.shape, LOW),
            jax.ShapeDtypeStruct((3, width), WIDE),
        ),
        in_specs=[pl.BlockSpec(memory_space=pltpu.SMEM)] + [whole] * len(operands),
        out_specs=[whole] * 5,
        scratch_shapes=[pltpu.VMEM((3, count, cols), WIDE), pltpu.VMEM((count, width), WIDE)],
        compiler_params=pltpu.CompilerParams(vmem_limit_bytes=56 * 2**20),
        name="home",
    )(me.astype(jnp.int32).reshape(1), *operands)


def expert_kernel(share, first, me_ref, *refs):
    own_ref, peer_ref, cot_own_ref, cot_peer_ref, router_ref, b_in_ref, b_out_ref = refs[:7]
    pieces, refs = (refs[7:9], refs[9:]) if first else (refs[7:11], refs[11:])
    added, refs = ((), refs) if first else (refs[:2], refs[2:])
    mine_ref, peers_ref, hidden_ref, d_pre_ref, d_rows_ref, sums_ref = refs[:6]
    rows, cots = refs[6:8]
    w_in, w_out = pieces if first else refs[8:]
    half = pl.program_id(0)

    @pl.when(half == 0)
    def _():
        rows[...] = own_ref[...]
        cots[...] = cot_own_ref[...]
        if not first:
            for full, top, low in ((w_in, *pieces[:2]), (w_out, *pieces[2:])):
                full[: top.shape[0]] = top[...]
                full[top.shape[0] :] = low[...]
        sums_ref[...] = jnp.zeros_like(sums_ref)

    @pl.when(half == 1)
    def _():
        rows[...] = peer_ref[...]
        cots[...] = cot_peer_ref[...]

    given = rows[...]
    logits = jnp.dot(given, router_ref[...], preferred_element_type=WIDE)
    powers = jnp.exp(logits - jnp.max(logits, axis=1, keepdims=True))
    mine = lax.broadcasted_iota(jnp.int32, powers.shape, 1) == me_ref[0]
    gate = jnp.sum(jnp.where(mine, powers, 0.0), axis=1, keepdims=True)
    gate = gate / jnp.sum(powers, axis=1, keepdims=True)
    d_wide = (gate * cots[...].astype(WIDE)).astype(LOW)
    d_rows_ref[...] = d_wide
    pre = jnp.dot(given, w_in[...], preferred_element_type=WIDE) + b_in_ref[...]
    below = 0.5 * (1.0 + lax.erf(pre * ROOT_HALF))
    hidden = (pre * below).astype(LOW)
    hidden_ref[...] = hidden
    slope = below + pre * (DENSITY * jnp.exp(-0.5 * pre * pre))
    d_hidden = lax.dot_general(d_wide, w_out[...], dims(1, 1), preferred_element_type=WIDE)
    d_pre = (d_hidden * slope).astype(LOW)
    d_pre_ref[...] = d_pre
    out = jnp.dot(hidden, w_out[...], preferred_element_type=WIDE)
    back = lax.dot_general(d_pre, w_in[...], dims(1, 1), preferred_element_type=WIDE)
    sums_ref[0:1] += jnp.sum(d_pre.astype(WIDE), axis=0, keepdims=True)
    d_sum = jnp.sum(d_wide.astype(WIDE), axis=0, keepdims=True)
    blocks = (out.shape[0] // share, share, out.shape[1])

    @pl.when(half == 0)
    def _():
        full = (out if first else out + b_out_ref[...]).reshape(blocks)
        pair = jnp.concatenate([full, back.reshape(blocks)], axis=1)
        mine_ref[...] = pair if first else pair + added[0][...]
        sums_ref[1:2] = d_sum

    @pl.when(half == 1)
    def _():
        pair = jnp.concatenate([out.reshape(blocks), back.reshape(blocks)], axis=1)
        peers_ref[...] = pair if first else (pair + added[1][...]).astype(LOW)
        sums_ref[2:3] = d_sum


def expert_work(share, me, rows, cots, router, b_in, b_out, w_in, w_out, added):
    count, width = rows[0].shape
    units = b_in.shape[1]
    first = not added
    operands = (*rows, *cots, router, b_in, b_out, *w_in, *w_out, *added)
    whole = [pl.BlockSpec(x.shape, lambda i, n=x.ndim: (0,) * n) for x in operands]
    moved = (count // share, 2 * share, width)
    each = lambda i: (i, 0)
    full = [] if first else [pltpu.VMEM((width, units), LOW), pltpu.VMEM((units, width), LOW)]
    return pl.pallas_call(
        functools.partial(expert_kernel, share, first),
        grid=(2,),
        out_shape=(
            jax.ShapeDtypeStruct(moved, WIDE),
            jax.ShapeDtypeStruct(moved, WIDE if first else LOW),
            jax.ShapeDtypeStruct((2 * count, units), LOW),
            jax.ShapeDtypeStruct((2 * count, units), LOW),
            jax.ShapeDtypeStruct((2 * count, width), LOW),
            jax.ShapeDtypeStruct((3, width), WIDE),
        ),
        in_specs=[pl.BlockSpec(memory_space=pltpu.SMEM)] + whole,
        out_specs=(
            pl.BlockSpec(moved, lambda i: (0, 0, 0)),
            pl.BlockSpec(moved, lambda i: (0, 0, 0)),
            pl.BlockSpec((count, units), each),
            pl.BlockSpec((count, units), each),
            pl.BlockSpec((count, width), each),
            pl.BlockSpec((3, width), lambda i: (0, 0)),
        ),
        scratch_shapes=[pltpu.VMEM((count, width), LOW)] * 2 + full,
        compiler_params=pltpu.CompilerParams(
            vmem_limit_bytes=52 * 2**20, dimension_semantics=("arbitrary",)
        ),
        name="expert_near" if first else "expert_far",
    )(me.astype(jnp.int32).reshape(1), *operands)


def on_device(
    tokens,
    ln1_gain,
    ln1_bias,
    w_qkv,
    b_qv,
    w_proj,
    b_proj,
    ln2_gain,
    ln2_bias,
    w_router,
    w_in,
    b_in,
    w_out,
    b_out,
    expert_ids,
    keep_mask,
    cotangent,
):
    tok_count, width = tokens.shape
    experts = w_router.shape[1]
    capacity = max(2, (2 * tok_count + experts - 1) // experts * 5 // 4)
    ranks = lax.axis_size("tensor")
    me_t, me_e = lax.axis_index("tensor"), lax.axis_index("expert")
    share = -(-capacity // (8 * ranks)) * 8
    local_cols = w_qkv.shape[2]
    order = tensor_order()

    far = ranks // 2
    cut = width // 2
    w_in_top, w_out_low = swap(w_in[0, :cut], far), swap(w_out[0, cut:], far)
    proj_all = placed_blocks(gather_list(w_proj), 0)

    ids = expert_ids.T
    kept = keep_mask.T > 0
    labels = jnp.arange(experts, dtype=jnp.int32)
    chosen = (ids[:, None, :] == labels[None, :, None])
    member = jnp.sum((chosen & kept[:, None, :]).astype(WIDE), axis=0)
    places = jnp.arange(tok_count, dtype=jnp.int32)
    earlier = (places[:, None] < places[None, :]).astype(LOW)
    before = dot_wide("et,ts->es", member.astype(LOW), earlier)
    slot = jnp.sum(jnp.where(chosen, before[None], 0.0), axis=1).astype(jnp.int32)
    holder = slot // share
    inner = ids * share + slot % share
    own_rows = experts * share
    own_place = jnp.where(kept & (holder == me_t), inner, -1)
    row_labels = jnp.arange(own_rows, dtype=jnp.int32)[:, None]
    own_hot = ((row_labels == own_place[0:1]) | (row_labels == own_place[1:2])).astype(LOW)
    all_place = jnp.where(kept, holder * own_rows + inner, -1).T
    all_labels = jnp.arange(ranks * own_rows, dtype=jnp.int32)[None, :]
    all_hot = ((all_labels == all_place[:, 0:1]) | (all_labels == all_place[:, 1:2])).astype(LOW)

    inputs = tokens.astype(WIDE)
    unit_one, scale_one = norm_parts(inputs)
    cot_rows = dot_wide("rt,td->rd", own_hot, cotangent.astype(LOW)).astype(LOW)
    own_tokens, cot_rows = together(tokens, cot_rows)
    cot_here = exchange(cot_rows)
    normed_low, triple, mixed_low = attend(own_tokens, ln1_gain, ln1_bias, w_qkv, b_qv)
    mixed_low, w_in_top = together(mixed_low, w_in_top)
    mixed_far = swap(mixed_low, far)
    mixed_far, w_in_rest = together(mixed_far, w_in[0, cut:])
    w_in_cuts = [w_in_top, swap(w_in_rest, far)]
    w_out_top = swap(w_out[0, :cut], far)
    mixed_all = placed_blocks(gather_list(mixed_low, mixed_far), 0)
    residual = inputs + (dot_wide("ct,cd->td", mixed_all, proj_all) + b_proj)
    unit_two, scale_two = norm_parts(residual)
    routed_low = (unit_two * ln2_gain + ln2_bias).astype(LOW)

    sent_rows = dot_wide("rt,td->rd", own_hot, routed_low).astype(LOW)
    sent_rows, cot_here, w_in_cuts[1] = together(sent_rows, cot_here, w_in_cuts[1])
    rows_here = exchange(sent_rows)
    rows_here, w_out_top = together(rows_here, w_out_top)
    rows_peer, b_in_far = swap(rows_here, 1), swap(b_in, far)
    rows_all = jnp.concatenate([rows_here, rows_peer], axis=0)
    shared = (share, me_e, (rows_here, rows_peer), (cot_here, swap(cot_here, 1)), w_router)
    far_out = (w_out_top, w_out_low)
    *added, near_hidden, near_pre, d_rows, near_sums = expert_work(
        *shared, b_in, b_out, (w_in[0],), (w_out[0],), ()
    )
    mine, peers, far_hidden, far_pre, _, far_sums = expert_work(
        *shared, b_in_far, b_out, w_in_cuts, far_out, added
    )
    hidden, d_pre = (near_hidden, far_hidden), (near_pre, far_pre)
    moved = exchange((mine + swap(peers, 1).astype(WIDE)).astype(LOW))

    far_out = dot_wide("rf,rd->fd", hidden[1], d_rows).astype(LOW)
    far_in = dot_wide("rd,rf->df", rows_all, d_pre[1]).astype(LOW)
    out_arrived = swap(far_out, far)
    near_out = dot_wide("rf,rd->fd", hidden[0], d_rows)
    near_in = dot_wide("rd,rf->df", rows_all, d_pre[0])
    d_sum = near_sums[1] + near_sums[2]
    other_sums = swap(jnp.stack([far_sums[0], d_sum]), far)

    route = jax.nn.softmax(dot_wide("de,td->et", w_router, routed_low), axis=0)
    hot_blocks = own_hot.reshape(experts, share, tok_count).astype(WIDE)
    slot_gate = jnp.sum(hot_blocks * route[:, None, :], axis=2).reshape(own_rows, 1)
    moved, out_arrived = together(moved, out_arrived)
    grad_w_out = near_out + out_arrived.astype(WIDE)
    out_home = moved[:, :share].reshape(own_rows, width)
    back_home = moved[:, share:].reshape(own_rows, width)
    slot_grad = jnp.sum(cot_rows.astype(WIDE) * out_home.astype(WIDE), axis=1)
    marks = jnp.concatenate(halves(slot_grad.reshape(experts, share)), axis=0)
    marks = jnp.pad(marks, ((0, 0), (0, -share % 128))).astype(LOW)
    back_blocks, marks = gather_list(back_home), gather_list(marks)
    gated = (slot_gate * out_home.astype(WIDE)).astype(LOW)
    back_blocks[1], gated, far_in = together(back_blocks[1], gated, far_in)
    mixture_part = dot_wide("rt,rd->td", own_hot, gated).astype(LOW)
    in_arrived = swap(far_in, far)
    d_residual, d_attn, d_triple, d_logits, sums = home(
        order,
        own_rows,
        share,
        me_t,
        back_blocks,
        marks,
        all_hot,
        route,
        w_router.T,
        residual,
        cotangent,
        ln2_gain,
        w_proj,
        triple,
    )
    grad_router = dot_wide("et,td->ed", d_logits, routed_low)
    grad_w_proj = dot_wide("ct,td->cd", mixed_low, d_attn)

    grad_w_qkv = dot_wide("jtc,td->jcd", d_triple, normed_low)
    grad_b_qv = jnp.stack(
        [jnp.sum(d_triple[0].astype(WIDE), axis=0), jnp.sum(d_triple[2].astype(WIDE), axis=0)]
    )
    d_normed_part = dot_wide("jtc,jdc->td", d_triple, w_qkv)
    grad_ln1_gain = jnp.sum(d_normed_part * unit_one, axis=0)
    grad_ln1_bias = jnp.sum(d_normed_part, axis=0)

    groups = lax.axis_size("expert")
    pair = jnp.pad(grad_b_qv.reshape(1, -1), ((0, 0), (0, width - 2 * local_cols)))
    small = jnp.stack([grad_ln1_gain, grad_ln1_bias])
    small = jnp.concatenate([small, sums, pair, grad_router], axis=0)
    count = small.shape[0]
    each = -(-count // groups)
    small = jnp.pad(small, ((0, groups * each - count), (0, 0))).reshape(groups, each, width)
    high, rest = halves(small)
    parts = grad_w_qkv.reshape(groups, -1, width)
    body = parts.shape[1]
    proj_parts = grad_w_proj.reshape(groups, -1, width)
    parts = jnp.concatenate([parts, proj_parts, high, rest], axis=1)
    proj_rows = proj_parts.shape[1]
    parts = jnp.pad(parts, ((0, 0), (0, -parts.shape[1] % 8), (0, 0)))
    parts, in_arrived, other_sums = together(parts, in_arrived, other_sums)
    grad_b_in = near_sums[0] + other_sums[0]
    grad_b_out = d_sum + other_sums[1]
    grad_w_in = near_in + in_arrived.astype(WIDE)

    rows_each = -(-tok_count // (16 * ranks)) * 16
    fill = ranks * rows_each - tok_count

    def rows_of(value, index):
        padded = jnp.pad(value, ((0, fill), (0, 0)))
        return lax.dynamic_slice_in_dim(padded, index * rows_each, rows_each, 0)

    both = jnp.concatenate([d_normed_part.astype(LOW), mixture_part], axis=1)
    shares = jnp.stack([rows_of(both, me_t ^ o) for o in order])
    shares = (shares[:2].astype(WIDE) + swap(shares[2:], 1).astype(WIDE)).astype(LOW)
    both = shares[0].astype(WIDE) + swap(shares[1], far).astype(WIDE)
    back = norm_back(
        rows_of(unit_one, me_t), rows_of(scale_one, me_t), ln1_gain, both[:, :width]
    )
    both = jnp.concatenate([back, both[:, width:]], axis=1).astype(LOW)

    def beside(done):
        pair, _ = together(both, done)
        pair = jnp.stack([pair, swap(pair, far)])
        pair = jnp.concatenate([pair, swap(pair, 1)], axis=0)
        full = jnp.zeros((ranks * rows_each, 2 * width), LOW)
        for place, o in enumerate(order):
            full = lax.dynamic_update_slice_in_dim(full, pair[place], (me_t ^ o) * rows_each, 0)
        full = full[:tok_count].astype(WIDE)
        return residual + full[:, width:], d_residual + full[:, :width]

    proj_sum, qkv_sum, small, (layer_out, grad_tokens) = expert_sum(
        parts, body, proj_rows, each, beside
    )
    proj_sum = proj_sum.reshape(local_cols, width)
    qkv_sum = jnp.swapaxes(qkv_sum.reshape(3, local_cols, width), 1, 2)
    small = small.reshape(groups * each, width)
    norm_sum = [small[:2]] + [swap(small[:2], step) for step in range(1, ranks)]
    norm_sum = (norm_sum[0] + norm_sum[1]) + sum(norm_sum[2:])
    return (
        layer_out,
        grad_tokens,
        norm_sum[0],
        norm_sum[1],
        qkv_sum,
        small[5, : 2 * local_cols].reshape(2, local_cols),
        proj_sum,
        small[4],
        small[2],
        small[3],
        small[6 : 6 + experts].T,
        grad_w_in[None],
        grad_b_in[None],
        grad_w_out[None],
        grad_b_out[None],
    )


def solution(mesh):
    placed = (
        P("expert", None),
        P(),
        P(),
        P(None, None, "tensor"),
        P(None, "tensor"),
        P("tensor", None),
        P(),
        P(),
        P(),
        P(),
        P("expert", None, "tensor"),
        P("expert", "tensor"),
        P("expert", "tensor", None),
        P("expert", None),
        P("expert", None),
        P("expert", None),
        P("expert", None),
    )
    return jax.shard_map(
        on_device,
        mesh=mesh,
        in_specs=placed,
        out_specs=(
            P("expert", None),
            P("expert", None),
            P(),
            P(),
            P(None, None, "tensor"),
            P(None, "tensor"),
            P("tensor", None),
            P(),
            P(),
            P(),
            P(),
            P("expert", None, "tensor"),
            P("expert", "tensor"),
            P("expert", "tensor", None),
            P("expert", None),
        ),
        check_vma=False,
    )
```

```python
import functools

import jax
import jax.numpy as jnp
from jax import lax
from jax.experimental import pallas as pl
from jax.experimental.pallas import tpu as pltpu
from jax.sharding import PartitionSpec as P

HEAD_DIM = 64
SEQ = 197
NORM_EPSILON = 1e-06
LOW = jnp.bfloat16
WIDE = jnp.float32
ROOT_HALF = 0.7071067811865476
DENSITY = 0.3989422804014327


def norm_parts(values):
    center = values - jnp.mean(values, axis=-1, keepdims=True)
    spread = jnp.mean(center * center, axis=-1, keepdims=True)
    scale = lax.rsqrt(spread + NORM_EPSILON)
    return center * scale, scale


def norm_back(unit, scale, gain_vec, grad):
    grad_unit = grad * gain_vec
    first = jnp.mean(grad_unit, axis=-1, keepdims=True)
    second = jnp.mean(grad_unit * unit, axis=-1, keepdims=True)
    return scale * (grad_unit - first - unit * second)


def dot_wide(equation, left, right):
    return jnp.einsum(equation, left, right, preferred_element_type=WIDE)


def swap(value, step):
    size = lax.axis_size("tensor")
    return lax.ppermute(value, "tensor", [(i, i ^ step) for i in range(size)])


def tensor_order():
    order, step = [0], lax.axis_size("tensor") // 2
    while step:
        order, step = order + [i ^ step for i in order], step // 2
    return order


def gather_list(block, far_block=None):
    blocks, step = [block], lax.axis_size("tensor") // 2
    if far_block is not None:
        blocks, step = [block, far_block], step // 2
    while step:
        blocks, step = blocks + [swap(b, step) for b in blocks], step // 2
    return blocks


def placed_blocks(blocks, axis):
    me, extent = lax.axis_index("tensor"), blocks[0].shape[axis]
    shape = list(blocks[0].shape)
    shape[axis] = extent * len(blocks)
    result = jnp.zeros(shape, blocks[0].dtype)
    for o, block in zip(tensor_order(), blocks):
        result = lax.dynamic_update_slice_in_dim(result, block, (me ^ o) * extent, axis)
    return result


def exchange(rows):
    return lax.all_to_all(rows, "expert", 0, 0, tiled=True)


def shift(value, step):
    size = lax.axis_size("expert")
    return lax.ppermute(value, "expert", [(i, (i + step) % size) for i in range(size)])


def unpack_kernel(body, proj, each, me_ref, *refs):
    size = len(refs) - 3
    proj_ref, qkv_ref, small_ref = refs[size:]
    for step in range(size):
        at = lax.rem(me_ref[0] + size - step, size)
        block = refs[step][...].astype(WIDE)
        qkv_ref[pl.ds(pl.multiple_of(at * body, 8), body), :] = block[:body]
        proj_ref[pl.ds(pl.multiple_of(at * proj, 8), proj), :] = block[body : body + proj]
        end = body + proj
        small_ref[at] = block[end : end + each] + block[end + each : end + 2 * each]


def expert_sum(parts, body, proj, each, beside):
    size, me = lax.axis_size("expert"), lax.axis_index("expert")
    width, end = parts.shape[2], body + proj
    if size > 8:
        total = lax.psum(parts, "expert")
        small = total[:, end : end + each] + total[:, end + each : end + 2 * each]
        return total[:, body:end], total[:, :body], small, beside(small)
    low = parts.astype(LOW)
    mine = lax.dynamic_index_in_dim(parts, me, 0, keepdims=False)
    moved = [
        shift(lax.dynamic_index_in_dim(low, (me + step) % size, 0, keepdims=False), step)
        for step in range(1, size)
    ]
    total = (mine + sum(part.astype(WIDE) for part in moved)).astype(LOW)
    blocks = [total] + [shift(total, step) for step in range(1, size)]
    others = beside(blocks[1])
    whole = pl.BlockSpec(memory_space=pltpu.VMEM)
    results = pl.pallas_call(
        functools.partial(unpack_kernel, body, proj, each),
        out_shape=(
            jax.ShapeDtypeStruct((size * proj, width), WIDE),
            jax.ShapeDtypeStruct((size * body, width), WIDE),
            jax.ShapeDtypeStruct((size, each, width), WIDE),
        ),
        in_specs=[pl.BlockSpec(memory_space=pltpu.SMEM)] + [whole] * size,
        out_specs=[whole] * 3,
        compiler_params=pltpu.CompilerParams(vmem_limit_bytes=40 * 2**20),
        name="unpack",
    )(me.astype(jnp.int32).reshape(1), *blocks)
    return *results, others


def halves(value):
    high = lax.reduce_precision(value, 8, 7)
    return high, value - high


def together(*values):
    return lax.optimization_barrier(values)


def dims(left, right):
    return (((left,), (right,)), ((), ()))


def low_dot(left, right, contract):
    return lax.dot_general(
        left.astype(LOW), right.astype(LOW), contract, preferred_element_type=WIDE
    )


def softmax_rows(queries, keys):
    scores = low_dot(queries, keys, dims(1, 1)) * HEAD_DIM ** (-0.5)
    powers = jnp.exp(scores - jnp.max(scores, axis=-1, keepdims=True))
    return powers / jnp.sum(powers, axis=-1, keepdims=True)


def attend_kernel(tok_ref, gain_ref, bias_ref, w_ref, b_ref, normed_ref, triple_ref, mixed_ref, hold):
    unit, _ = norm_parts(tok_ref[...].astype(WIDE))
    normed = (unit * gain_ref[...] + bias_ref[...]).astype(LOW)
    normed_ref[...] = normed
    cols = w_ref.shape[1]
    for j in range(3):
        part = lax.dot_general(normed, w_ref[j], dims(1, 1), preferred_element_type=WIDE)
        if j != 1:
            part = part + b_ref[j // 2 : j // 2 + 1, :]
        part = part.astype(LOW)
        triple_ref[j] = part
        hold[j] = part.astype(WIDE)
    for i in range(tok_ref.shape[0] // SEQ):
        rows = pl.ds(i * SEQ, SEQ)
        queries, keys, values = hold[0, rows, :], hold[1, rows, :], hold[2, rows, :]
        parts = []
        for at in range(0, cols, HEAD_DIM):
            head = slice(at, at + HEAD_DIM)
            probs = softmax_rows(queries[:, head], keys[:, head])
            parts.append(low_dot(probs, values[:, head], dims(1, 0)))
        hold[0, rows, :] = jnp.concatenate(parts, axis=1)
    mixed_ref[...] = hold[0].T.astype(LOW)


def attend(tokens, gain, bias, w_qkv, b_qv):
    count, width = tokens.shape
    cols = w_qkv.shape[2]
    return pl.pallas_call(
        attend_kernel,
        out_shape=(
            jax.ShapeDtypeStruct((count, width), LOW),
            jax.ShapeDtypeStruct((3, count, cols), LOW),
            jax.ShapeDtypeStruct((cols, count), LOW),
        ),
        scratch_shapes=[pltpu.VMEM((3, count, cols), WIDE)],
        compiler_params=pltpu.CompilerParams(vmem_limit_bytes=40 * 2**20),
        name="attend",
    )(tokens, gain[None], bias[None], jnp.swapaxes(w_qkv, 1, 2), b_qv)


def attend_back(queries, keys, values, grads):
    factor = HEAD_DIM ** (-0.5)
    parts = [[], [], []]
    for at in range(0, queries.shape[1], HEAD_DIM):
        head = slice(at, at + HEAD_DIM)
        q, k, v, g = queries[:, head], keys[:, head], values[:, head], grads[:, head]
        probs = softmax_rows(q, k)
        d_probs = low_dot(g, v, dims(1, 1))
        d_scores = probs * (d_probs - jnp.sum(probs * d_probs, axis=-1, keepdims=True))
        parts[0].append(low_dot(d_scores, k, dims(1, 0)) * factor)
        parts[1].append(low_dot(d_scores, q, dims(0, 0)) * factor)
        parts[2].append(low_dot(probs, g, dims(0, 0)))
    return [jnp.concatenate(p, axis=1) for p in parts]


def home_kernel(order, own_rows, share, me_ref, *refs):
    ranks = len(order)
    blocks, marks, refs = refs[:ranks], refs[ranks : 2 * ranks], refs[2 * ranks :]
    hot_ref, route_ref, router_ref, res_ref, cot_ref, gain_ref, proj_ref, triple_ref = refs[:8]
    d_res_ref, d_attn_ref, d_triple_ref, d_logits_ref, sums_ref, hold, total = refs[8:]
    experts = route_ref.shape[0]
    spread = 0.0
    line = lax.broadcasted_iota(jnp.int32, (2 * experts, own_rows), 0) % experts
    mask = line == lax.broadcasted_iota(jnp.int32, (2 * experts, own_rows), 1) // share
    for p, o in enumerate(order):
        start = pl.multiple_of((me_ref[0] ^ o) * own_rows, own_rows)
        hot = hot_ref[:, pl.ds(start, own_rows)]
        part = jnp.dot(hot, blocks[p][...], preferred_element_type=WIDE)
        total[...] = part if p == 0 else total[...] + part
        mark = marks[p][...].astype(WIDE)[:, :share]
        mark = jnp.where(mask, jnp.concatenate([mark] * experts, axis=1), 0.0)
        spread = spread + low_dot(mark, hot, dims(1, 1))
    d_route = spread[:experts] + spread[experts:]
    route = route_ref[...]
    inner = jnp.sum(d_route * route, axis=0, keepdims=True)
    d_logits = (route * (d_route - inner)).astype(LOW)
    d_logits_ref[...] = d_logits
    total[...] += low_dot(d_logits, router_ref[...], dims(0, 0))
    for j in range(3):
        hold[j] = triple_ref[j].astype(WIDE)
    sums = [0.0, 0.0, 0.0]
    for i in range(res_ref.shape[0] // SEQ):
        rows = pl.ds(i * SEQ, SEQ)
        d_routed = total[rows, :]
        unit, scale = norm_parts(res_ref[rows, :])
        d_residual = cot_ref[rows, :] + norm_back(unit, scale, gain_ref[...], d_routed)
        d_res_ref[rows, :] = d_residual
        d_attn = d_residual.astype(LOW)
        wide = d_attn.astype(WIDE)
        total[rows, :] = wide
        for n, term in enumerate((d_routed * unit, d_routed, wide)):
            sums[n] = sums[n] + jnp.sum(term, axis=0, keepdims=True)
        d_mixed = lax.dot_general(d_attn, proj_ref[...], dims(1, 1), preferred_element_type=WIDE)
        d_mixed = d_mixed.astype(LOW).astype(WIDE)
        parts = attend_back(hold[0, rows, :], hold[1, rows, :], hold[2, rows, :], d_mixed)
        for j in range(3):
            hold[j, rows, :] = parts[j]
    d_attn_ref[...] = total[...].astype(LOW)
    for j in range(3):
        d_triple_ref[j] = hold[j].astype(LOW)
    sums_ref[...] = jnp.concatenate(sums, axis=0)


def home(order, own_rows, share, me, blocks, marks, hot, route, router, res, cot, gain, proj, triple):
    _, count, cols = triple.shape
    width = res.shape[1]
    kernel = functools.partial(home_kernel, order, own_rows, share)
    whole = pl.BlockSpec(memory_space=pltpu.VMEM)
    operands = (*blocks, *marks, hot, route, router, res, cot, gain[None], proj, triple)
    return pl.pallas_call(
        kernel,
        out_shape=(
            jax.ShapeDtypeStruct((count, width), WIDE),
            jax.ShapeDtypeStruct((count, width), LOW),
            jax.ShapeDtypeStruct(triple.shape, LOW),
            jax.ShapeDtypeStruct(route.shape, LOW),
            jax.ShapeDtypeStruct((3, width), WIDE),
        ),
        in_specs=[pl.BlockSpec(memory_space=pltpu.SMEM)] + [whole] * len(operands),
        out_specs=[whole] * 5,
        scratch_shapes=[pltpu.VMEM((3, count, cols), WIDE), pltpu.VMEM((count, width), WIDE)],
        compiler_params=pltpu.CompilerParams(vmem_limit_bytes=56 * 2**20),
        name="home",
    )(me.astype(jnp.int32).reshape(1), *operands)


def expert_kernel(share, first, me_ref, *refs):
    own_ref, peer_ref, cot_own_ref, cot_peer_ref, router_ref, b_in_ref, b_out_ref = refs[:7]
    pieces, refs = (refs[7:9], refs[9:]) if first else (refs[7:11], refs[11:])
    added, refs = ((), refs) if first else (refs[:2], refs[2:])
    mine_ref, peers_ref, hidden_ref, d_pre_ref, sums_ref = refs[:5]
    rows, cots = refs[6:8] if first else refs[5:7]
    w_in, w_out = pieces if first else refs[7:]
    half = pl.program_id(0)

    @pl.when(half == 0)
    def _():
        rows[...] = own_ref[...]
        cots[...] = cot_own_ref[...]
        if not first:
            for full, top, low in ((w_in, *pieces[:2]), (w_out, *pieces[2:])):
                full[: top.shape[0]] = top[...]
                full[top.shape[0] :] = low[...]
        sums_ref[...] = jnp.zeros_like(sums_ref)

    @pl.when(half == 1)
    def _():
        rows[...] = peer_ref[...]
        cots[...] = cot_peer_ref[...]

    given = rows[...]
    logits = jnp.dot(given, router_ref[...], preferred_element_type=WIDE)
    powers = jnp.exp(logits - jnp.max(logits, axis=1, keepdims=True))
    mine = lax.broadcasted_iota(jnp.int32, powers.shape, 1) == me_ref[0]
    gate = jnp.sum(jnp.where(mine, powers, 0.0), axis=1, keepdims=True)
    gate = gate / jnp.sum(powers, axis=1, keepdims=True)
    d_wide = (gate * cots[...].astype(WIDE)).astype(LOW)
    if first:
        refs[5][...] = d_wide
    pre = jnp.dot(given, w_in[...], preferred_element_type=WIDE) + b_in_ref[...]
    below = 0.5 * (1.0 + lax.erf(pre * ROOT_HALF))
    hidden = (pre * below).astype(LOW)
    hidden_ref[...] = hidden
    slope = below + pre * (DENSITY * jnp.exp(-0.5 * pre * pre))
    d_hidden = lax.dot_general(d_wide, w_out[...], dims(1, 1), preferred_element_type=WIDE)
    d_pre = (d_hidden * slope).astype(LOW)
    d_pre_ref[...] = d_pre
    out = jnp.dot(hidden, w_out[...], preferred_element_type=WIDE)
    back = lax.dot_general(d_pre, w_in[...], dims(1, 1), preferred_element_type=WIDE)
    sums_ref[0:1] += jnp.sum(d_pre.astype(WIDE), axis=0, keepdims=True)
    d_sum = jnp.sum(d_wide.astype(WIDE), axis=0, keepdims=True)
    blocks = (out.shape[0] // share, share, out.shape[1])

    @pl.when(half == 0)
    def _():
        full = (out if first else out + b_out_ref[...]).reshape(blocks)
        pair = jnp.concatenate([full, back.reshape(blocks)], axis=1)
        mine_ref[...] = (pair if first else pair + added[0][...].astype(WIDE)).astype(LOW)
        sums_ref[1:2] = d_sum

    @pl.when(half == 1)
    def _():
        pair = jnp.concatenate([out.reshape(blocks), back.reshape(blocks)], axis=1)
        peers_ref[...] = (pair if first else pair + added[1][...].astype(WIDE)).astype(LOW)
        sums_ref[2:3] = d_sum


def expert_work(share, me, rows, cots, router, b_in, b_out, w_in, w_out, added):
    count, width = rows[0].shape
    units = b_in.shape[1]
    first = not added
    operands = (*rows, *cots, router, b_in, b_out, *w_in, *w_out, *added)
    whole = [pl.BlockSpec(x.shape, lambda i, n=x.ndim: (0,) * n) for x in operands]
    moved = (count // share, 2 * share, width)
    each = lambda i: (i, 0)
    full = [] if first else [pltpu.VMEM((width, units), LOW), pltpu.VMEM((units, width), LOW)]
    return pl.pallas_call(
        functools.partial(expert_kernel, share, first),
        grid=(2,),
        out_shape=(
            jax.ShapeDtypeStruct(moved, LOW),
            jax.ShapeDtypeStruct(moved, LOW),
            jax.ShapeDtypeStruct((2 * count, units), LOW),
            jax.ShapeDtypeStruct((2 * count, units), LOW),
            jax.ShapeDtypeStruct((3, width), WIDE),
            jax.ShapeDtypeStruct((2 * count, width), LOW),
        )[: 6 if first else 5],
        in_specs=[pl.BlockSpec(memory_space=pltpu.SMEM)] + whole,
        out_specs=(
            pl.BlockSpec(moved, lambda i: (0, 0, 0)),
            pl.BlockSpec(moved, lambda i: (0, 0, 0)),
            pl.BlockSpec((count, units), each),
            pl.BlockSpec((count, units), each),
            pl.BlockSpec((3, width), lambda i: (0, 0)),
            pl.BlockSpec((count, width), each),
        )[: 6 if first else 5],
        scratch_shapes=[pltpu.VMEM((count, width), LOW)] * 2 + full,
        compiler_params=pltpu.CompilerParams(
            vmem_limit_bytes=52 * 2**20, dimension_semantics=("arbitrary",)
        ),
        name="expert_near" if first else "expert_far",
    )(me.astype(jnp.int32).reshape(1), *operands)


def on_device(
    tokens,
    ln1_gain,
    ln1_bias,
    w_qkv,
    b_qv,
    w_proj,
    b_proj,
    ln2_gain,
    ln2_bias,
    w_router,
    w_in,
    b_in,
    w_out,
    b_out,
    expert_ids,
    keep_mask,
    cotangent,
):
    tok_count, width = tokens.shape
    experts = w_router.shape[1]
    capacity = max(2, (2 * tok_count + experts - 1) // experts * 5 // 4)
    ranks = lax.axis_size("tensor")
    me_t, me_e = lax.axis_index("tensor"), lax.axis_index("expert")
    share = -(-capacity // (8 * ranks)) * 8
    local_cols = w_qkv.shape[2]
    order = tensor_order()

    far = ranks // 2
    cut = width // 2
    w_in_top, w_out_low = swap(w_in[0, :cut], far), swap(w_out[0, cut:], far)
    proj_all = placed_blocks(gather_list(w_proj), 0)

    ids = expert_ids.T
    kept = keep_mask.T > 0
    labels = jnp.arange(experts, dtype=jnp.int32)
    chosen = (ids[:, None, :] == labels[None, :, None])
    member = jnp.sum((chosen & kept[:, None, :]).astype(WIDE), axis=0)
    places = jnp.arange(tok_count, dtype=jnp.int32)
    earlier = (places[:, None] < places[None, :]).astype(LOW)
    before = dot_wide("et,ts->es", member.astype(LOW), earlier)
    slot = jnp.sum(jnp.where(chosen, before[None], 0.0), axis=1).astype(jnp.int32)
    holder = slot // share
    inner = ids * share + slot % share
    own_rows = experts * share
    own_place = jnp.where(kept & (holder == me_t), inner, -1)
    row_labels = jnp.arange(own_rows, dtype=jnp.int32)[:, None]
    own_hot = ((row_labels == own_place[0:1]) | (row_labels == own_place[1:2])).astype(LOW)
    all_place = jnp.where(kept, holder * own_rows + inner, -1).T
    all_labels = jnp.arange(ranks * own_rows, dtype=jnp.int32)[None, :]
    all_hot = ((all_labels == all_place[:, 0:1]) | (all_labels == all_place[:, 1:2])).astype(LOW)

    inputs = tokens.astype(WIDE)
    unit_one, scale_one = norm_parts(inputs)
    cot_rows = dot_wide("rt,td->rd", own_hot, cotangent.astype(LOW)).astype(LOW)
    own_tokens, cot_rows = together(tokens, cot_rows)
    cot_here = exchange(cot_rows)
    normed_low, triple, mixed_low = attend(own_tokens, ln1_gain, ln1_bias, w_qkv, b_qv)
    mixed_low, w_in_top = together(mixed_low, w_in_top)
    mixed_far = swap(mixed_low, far)
    mixed_far, w_in_rest = together(mixed_far, w_in[0, cut:])
    w_in_cuts = [w_in_top, swap(w_in_rest, far)]
    w_out_top = swap(w_out[0, :cut], far)
    mixed_all = placed_blocks(gather_list(mixed_low, mixed_far), 0)
    residual = inputs + (dot_wide("ct,cd->td", mixed_all, proj_all) + b_proj)
    unit_two, scale_two = norm_parts(residual)
    routed_low = (unit_two * ln2_gain + ln2_bias).astype(LOW)

    sent_rows = dot_wide("rt,td->rd", own_hot, routed_low).astype(LOW)
    sent_rows, cot_here, w_in_cuts[1] = together(sent_rows, cot_here, w_in_cuts[1])
    rows_here = exchange(sent_rows)
    rows_here, w_out_top = together(rows_here, w_out_top)
    rows_peer, b_in_far = swap(rows_here, 1), swap(b_in, far)
    rows_all = jnp.concatenate([rows_here, rows_peer], axis=0)
    shared = (share, me_e, (rows_here, rows_peer), (cot_here, swap(cot_here, 1)), w_router)
    far_out = (w_out_top, w_out_low)
    *added, near_hidden, near_pre, near_sums, d_rows = expert_work(
        *shared, b_in, b_out, (w_in[0],), (w_out[0],), ()
    )
    mine, peers, far_hidden, far_pre, far_sums = expert_work(
        *shared, b_in_far, b_out, w_in_cuts, far_out, added
    )
    hidden, d_pre = (near_hidden, far_hidden), (near_pre, far_pre)
    moved = exchange((mine.astype(WIDE) + swap(peers, 1).astype(WIDE)).astype(LOW))

    far_out = dot_wide("rf,rd->fd", hidden[1], d_rows).astype(LOW)
    far_in = dot_wide("rd,rf->df", rows_all, d_pre[1]).astype(LOW)
    out_arrived = swap(far_out, far)
    near_out = dot_wide("rf,rd->fd", hidden[0], d_rows)
    near_in = dot_wide("rd,rf->df", rows_all, d_pre[0])
    d_sum = near_sums[1] + near_sums[2]
    other_sums = swap(jnp.stack([far_sums[0], d_sum]), far)

    route = jax.nn.softmax(dot_wide("de,td->et", w_router, routed_low), axis=0)
    hot_blocks = own_hot.reshape(experts, share, tok_count).astype(WIDE)
    slot_gate = jnp.sum(hot_blocks * route[:, None, :], axis=2).reshape(own_rows, 1)
    moved, out_arrived, far_in = together(moved, out_arrived, far_in)
    grad_w_out = near_out + out_arrived.astype(WIDE)
    out_home = moved[:, :share].reshape(own_rows, width)
    back_home = moved[:, share:].reshape(own_rows, width)
    slot_grad = jnp.sum(cot_rows.astype(WIDE) * out_home.astype(WIDE), axis=1)
    marks = jnp.concatenate(halves(slot_grad.reshape(experts, share)), axis=0)
    marks = jnp.pad(marks, ((0, 0), (0, -share % 128))).astype(LOW)
    back_far, marks_far = together(swap(back_home, far), swap(marks, far))
    back_blocks, marks = gather_list(back_home, back_far), gather_list(marks, marks_far)
    gated = (slot_gate * out_home.astype(WIDE)).astype(LOW)
    back_blocks[1], gated, far_in = together(back_blocks[1], gated, far_in)
    mixture_part = dot_wide("rt,rd->td", own_hot, gated).astype(LOW)
    in_arrived = swap(far_in, far)
    d_residual, d_attn, d_triple, d_logits, sums = home(
        order,
        own_rows,
        share,
        me_t,
        back_blocks,
        marks,
        all_hot,
        route,
        w_router.T,
        residual,
        cotangent,
        ln2_gain,
        w_proj,
        triple,
    )
    grad_router = dot_wide("et,td->ed", d_logits, routed_low)
    grad_w_proj = dot_wide("ct,td->cd", mixed_low, d_attn)

    grad_w_qkv = dot_wide("jtc,td->jcd", d_triple, normed_low)
    grad_b_qv = jnp.stack(
        [jnp.sum(d_triple[0].astype(WIDE), axis=0), jnp.sum(d_triple[2].astype(WIDE), axis=0)]
    )
    d_normed_part = dot_wide("jtc,jdc->td", d_triple, w_qkv)
    grad_ln1_gain = jnp.sum(d_normed_part * unit_one, axis=0)
    grad_ln1_bias = jnp.sum(d_normed_part, axis=0)

    groups = lax.axis_size("expert")
    pair = jnp.pad(grad_b_qv.reshape(1, -1), ((0, 0), (0, width - 2 * local_cols)))
    small = jnp.stack([grad_ln1_gain, grad_ln1_bias])
    small = jnp.concatenate([small, sums, pair, grad_router], axis=0)
    count = small.shape[0]
    each = -(-count // groups)
    small = jnp.pad(small, ((0, groups * each - count), (0, 0))).reshape(groups, each, width)
    high, rest = halves(small)
    parts = grad_w_qkv.reshape(groups, -1, width)
    body = parts.shape[1]
    proj_parts = grad_w_proj.reshape(groups, -1, width)
    parts = jnp.concatenate([parts, proj_parts, high, rest], axis=1)
    proj_rows = proj_parts.shape[1]
    parts = jnp.pad(parts, ((0, 0), (0, -parts.shape[1] % 8), (0, 0)))
    parts, in_arrived, other_sums = together(parts, in_arrived, other_sums)
    grad_b_in = near_sums[0] + other_sums[0]
    grad_b_out = d_sum + other_sums[1]
    grad_w_in = near_in + in_arrived.astype(WIDE)

    rows_each = -(-tok_count // (16 * ranks)) * 16
    fill = ranks * rows_each - tok_count

    def rows_of(value, index):
        padded = jnp.pad(value, ((0, fill), (0, 0)))
        return lax.dynamic_slice_in_dim(padded, index * rows_each, rows_each, 0)

    both = jnp.concatenate([d_normed_part.astype(LOW), mixture_part], axis=1)
    shares = jnp.stack([rows_of(both, me_t ^ o) for o in order])
    shares = (shares[:2].astype(WIDE) + swap(shares[2:], 1).astype(WIDE)).astype(LOW)
    both = shares[0].astype(WIDE) + swap(shares[1], far).astype(WIDE)
    back = norm_back(
        rows_of(unit_one, me_t), rows_of(scale_one, me_t), ln1_gain, both[:, :width]
    )
    both = jnp.concatenate([back, both[:, width:]], axis=1).astype(LOW)

    def beside(done):
        pair, _ = together(both, done)
        pair = jnp.stack([pair, swap(pair, far)])
        pair = jnp.concatenate([pair, swap(pair, 1)], axis=0)
        full = jnp.zeros((ranks * rows_each, 2 * width), LOW)
        for place, o in enumerate(order):
            full = lax.dynamic_update_slice_in_dim(full, pair[place], (me_t ^ o) * rows_each, 0)
        full = full[:tok_count].astype(WIDE)
        return residual + full[:, width:], d_residual + full[:, :width]

    proj_sum, qkv_sum, small, (layer_out, grad_tokens) = expert_sum(
        parts, body, proj_rows, each, beside
    )
    proj_sum = proj_sum.reshape(local_cols, width)
    qkv_sum = jnp.swapaxes(qkv_sum.reshape(3, local_cols, width), 1, 2)
    small = small.reshape(groups * each, width)
    norm_sum = [small[:2]] + [swap(small[:2], step) for step in range(1, ranks)]
    norm_sum = (norm_sum[0] + norm_sum[1]) + sum(norm_sum[2:])
    return (
        layer_out,
        grad_tokens,
        norm_sum[0],
        norm_sum[1],
        qkv_sum,
        small[5, : 2 * local_cols].reshape(2, local_cols),
        proj_sum,
        small[4],
        small[2],
        small[3],
        small[6 : 6 + experts].T,
        grad_w_in[None],
        grad_b_in[None],
        grad_w_out[None],
        grad_b_out[None],
    )


def solution(mesh):
    placed = (
        P("expert", None),
        P(),
        P(),
        P(None, None, "tensor"),
        P(None, "tensor"),
        P("tensor", None),
        P(),
        P(),
        P(),
        P(),
        P("expert", None, "tensor"),
        P("expert", "tensor"),
        P("expert", "tensor", None),
        P("expert", None),
        P("expert", None),
        P("expert", None),
        P("expert", None),
    )
    return jax.shard_map(
        on_device,
        mesh=mesh,
        in_specs=placed,
        out_specs=(
            P("expert", None),
            P("expert", None),
            P(),
            P(),
            P(None, None, "tensor"),
            P(None, "tensor"),
            P("tensor", None),
            P(),
            P(),
            P(),
            P(),
            P("expert", None, "tensor"),
            P("expert", "tensor"),
            P("expert", "tensor", None),
            P("expert", None),
        ),
        check_vma=False,
    )
```

```python
import functools

import jax
import jax.numpy as jnp
from jax import lax
from jax.experimental import pallas as pl
from jax.experimental.pallas import tpu as pltpu
from jax.sharding import PartitionSpec as P

HEAD_DIM = 64
SEQ = 197
NORM_EPSILON = 1e-06
LOW = jnp.bfloat16
WIDE = jnp.float32
ROOT_HALF = 0.7071067811865476
DENSITY = 0.3989422804014327


def norm_parts(values):
    center = values - jnp.mean(values, axis=-1, keepdims=True)
    spread = jnp.mean(center * center, axis=-1, keepdims=True)
    scale = lax.rsqrt(spread + NORM_EPSILON)
    return center * scale, scale


def norm_back(unit, scale, gain_vec, grad):
    grad_unit = grad * gain_vec
    first = jnp.mean(grad_unit, axis=-1, keepdims=True)
    second = jnp.mean(grad_unit * unit, axis=-1, keepdims=True)
    return scale * (grad_unit - first - unit * second)


def dot_wide(equation, left, right):
    return jnp.einsum(equation, left, right, preferred_element_type=WIDE)


def swap(value, step):
    size = lax.axis_size("tensor")
    return lax.ppermute(value, "tensor", [(i, i ^ step) for i in range(size)])


def tensor_order():
    order, step = [0], lax.axis_size("tensor") // 2
    while step:
        order, step = order + [i ^ step for i in order], step // 2
    return order


def gather_list(block, far_block=None):
    blocks, step = [block], lax.axis_size("tensor") // 2
    if far_block is not None:
        blocks, step = [block, far_block], step // 2
    while step:
        blocks, step = blocks + [swap(b, step) for b in blocks], step // 2
    return blocks


def placed_blocks(blocks, axis):
    me, extent = lax.axis_index("tensor"), blocks[0].shape[axis]
    shape = list(blocks[0].shape)
    shape[axis] = extent * len(blocks)
    result = jnp.zeros(shape, blocks[0].dtype)
    for o, block in zip(tensor_order(), blocks):
        result = lax.dynamic_update_slice_in_dim(result, block, (me ^ o) * extent, axis)
    return result


def exchange(rows):
    return lax.all_to_all(rows, "expert", 0, 0, tiled=True)


def shift(value, step):
    size = lax.axis_size("expert")
    return lax.ppermute(value, "expert", [(i, (i + step) % size) for i in range(size)])


def unpack_kernel(body, proj, each, me_ref, *refs):
    size = len(refs) - 3
    proj_ref, qkv_ref, small_ref = refs[size:]
    for step in range(size):
        at = lax.rem(me_ref[0] + size - step, size)
        block = refs[step][...].astype(WIDE)
        qkv_ref[pl.ds(pl.multiple_of(at * body, 8), body), :] = block[:body]
        proj_ref[pl.ds(pl.multiple_of(at * proj, 8), proj), :] = block[body : body + proj]
        end = body + proj
        small_ref[at] = block[end : end + each] + block[end + each : end + 2 * each]


def expert_sum(parts, body, proj, each, beside):
    size, me = lax.axis_size("expert"), lax.axis_index("expert")
    width, end = parts.shape[2], body + proj
    if size > 8:
        total = lax.psum(parts, "expert")
        small = total[:, end : end + each] + total[:, end + each : end + 2 * each]
        return total[:, body:end], total[:, :body], small, beside(small)
    low = parts.astype(LOW)
    mine = lax.dynamic_index_in_dim(parts, me, 0, keepdims=False)
    moved = [
        shift(lax.dynamic_index_in_dim(low, (me + step) % size, 0, keepdims=False), step)
        for step in range(1, size)
    ]
    total = (mine + sum(part.astype(WIDE) for part in moved)).astype(LOW)
    blocks = [total] + [shift(total, step) for step in range(1, size)]
    others = beside(blocks[1])
    whole = pl.BlockSpec(memory_space=pltpu.VMEM)
    results = pl.pallas_call(
        functools.partial(unpack_kernel, body, proj, each),
        out_shape=(
            jax.ShapeDtypeStruct((size * proj, width), WIDE),
            jax.ShapeDtypeStruct((size * body, width), WIDE),
            jax.ShapeDtypeStruct((size, each, width), WIDE),
        ),
        in_specs=[pl.BlockSpec(memory_space=pltpu.SMEM)] + [whole] * size,
        out_specs=[whole] * 3,
        compiler_params=pltpu.CompilerParams(vmem_limit_bytes=40 * 2**20),
        name="unpack",
    )(me.astype(jnp.int32).reshape(1), *blocks)
    return *results, others


def halves(value):
    high = lax.reduce_precision(value, 8, 7)
    return high, value - high


def together(*values):
    return lax.optimization_barrier(values)


def dims(left, right):
    return (((left,), (right,)), ((), ()))


def low_dot(left, right, contract):
    return lax.dot_general(
        left.astype(LOW), right.astype(LOW), contract, preferred_element_type=WIDE
    )


def softmax_rows(queries, keys):
    scores = low_dot(queries, keys, dims(1, 1)) * HEAD_DIM ** (-0.5)
    powers = jnp.exp(scores - jnp.max(scores, axis=-1, keepdims=True))
    return powers / jnp.sum(powers, axis=-1, keepdims=True)


def attend_kernel(tok_ref, gain_ref, bias_ref, w_ref, b_ref, normed_ref, triple_ref, mixed_ref, hold):
    unit, _ = norm_parts(tok_ref[...].astype(WIDE))
    normed = (unit * gain_ref[...] + bias_ref[...]).astype(LOW)
    normed_ref[...] = normed
    cols = w_ref.shape[1]
    for j in range(3):
        part = lax.dot_general(normed, w_ref[j], dims(1, 1), preferred_element_type=WIDE)
        if j != 1:
            part = part + b_ref[j // 2 : j // 2 + 1, :]
        part = part.astype(LOW)
        triple_ref[j] = part
        hold[j] = part.astype(WIDE)
    for i in range(tok_ref.shape[0] // SEQ):
        rows = pl.ds(i * SEQ, SEQ)
        queries, keys, values = hold[0, rows, :], hold[1, rows, :], hold[2, rows, :]
        parts = []
        for at in range(0, cols, HEAD_DIM):
            head = slice(at, at + HEAD_DIM)
            probs = softmax_rows(queries[:, head], keys[:, head])
            parts.append(low_dot(probs, values[:, head], dims(1, 0)))
        hold[0, rows, :] = jnp.concatenate(parts, axis=1)
    mixed_ref[...] = hold[0].T.astype(LOW)


def attend(tokens, gain, bias, w_qkv, b_qv):
    count, width = tokens.shape
    cols = w_qkv.shape[2]
    return pl.pallas_call(
        attend_kernel,
        out_shape=(
            jax.ShapeDtypeStruct((count, width), LOW),
            jax.ShapeDtypeStruct((3, count, cols), LOW),
            jax.ShapeDtypeStruct((cols, count), LOW),
        ),
        scratch_shapes=[pltpu.VMEM((3, count, cols), WIDE)],
        compiler_params=pltpu.CompilerParams(vmem_limit_bytes=40 * 2**20),
        name="attend",
    )(tokens, gain[None], bias[None], jnp.swapaxes(w_qkv, 1, 2), b_qv)


def attend_back(queries, keys, values, grads):
    factor = HEAD_DIM ** (-0.5)
    parts = [[], [], []]
    for at in range(0, queries.shape[1], HEAD_DIM):
        head = slice(at, at + HEAD_DIM)
        q, k, v, g = queries[:, head], keys[:, head], values[:, head], grads[:, head]
        probs = softmax_rows(q, k)
        d_probs = low_dot(g, v, dims(1, 1))
        d_scores = probs * (d_probs - jnp.sum(probs * d_probs, axis=-1, keepdims=True))
        parts[0].append(low_dot(d_scores, k, dims(1, 0)) * factor)
        parts[1].append(low_dot(d_scores, q, dims(0, 0)) * factor)
        parts[2].append(low_dot(probs, g, dims(0, 0)))
    return [jnp.concatenate(p, axis=1) for p in parts]


def home_kernel(order, own_rows, share, me_ref, *refs):
    ranks = len(order)
    blocks, marks, refs = refs[:ranks], refs[ranks : 2 * ranks], refs[2 * ranks :]
    hot_ref, route_ref, router_ref, res_ref, cot_ref, gain_ref, proj_ref, triple_ref = refs[:8]
    d_res_ref, d_attn_ref, d_triple_ref, d_logits_ref, sums_ref, hold, total, back, spread = refs[8:]
    experts = route_ref.shape[0]
    line = lax.broadcasted_iota(jnp.int32, (2 * experts, own_rows), 0) % experts
    mask = line == lax.broadcasted_iota(jnp.int32, (2 * experts, own_rows), 1) // share
    for p, o in enumerate(order):
        start = pl.multiple_of((me_ref[0] ^ o) * own_rows, own_rows)
        back[pl.ds(start, own_rows), :] = blocks[p][...]
        mark = marks[p][...].astype(WIDE)[:, :share]
        mark = jnp.where(mask, jnp.concatenate([mark] * experts, axis=1), 0.0)
        spread[:, pl.ds(start, own_rows)] = mark.astype(LOW)
    total[...] = jnp.dot(hot_ref[...], back[...], preferred_element_type=WIDE)
    d_route = low_dot(spread[...], hot_ref[...], dims(1, 1))
    d_route = d_route[:experts] + d_route[experts:]
    route = route_ref[...]
    inner = jnp.sum(d_route * route, axis=0, keepdims=True)
    d_logits = (route * (d_route - inner)).astype(LOW)
    d_logits_ref[...] = d_logits
    total[...] += low_dot(d_logits, router_ref[...], dims(0, 0))
    for j in range(3):
        hold[j] = triple_ref[j].astype(WIDE)
    sums = [0.0, 0.0, 0.0]
    for i in range(res_ref.shape[0] // SEQ):
        rows = pl.ds(i * SEQ, SEQ)
        d_routed = total[rows, :]
        unit, scale = norm_parts(res_ref[rows, :])
        d_residual = cot_ref[rows, :] + norm_back(unit, scale, gain_ref[...], d_routed)
        d_res_ref[rows, :] = d_residual
        d_attn = d_residual.astype(LOW)
        wide = d_attn.astype(WIDE)
        total[rows, :] = wide
        for n, term in enumerate((d_routed * unit, d_routed, wide)):
            sums[n] = sums[n] + jnp.sum(term, axis=0, keepdims=True)
        d_mixed = lax.dot_general(d_attn, proj_ref[...], dims(1, 1), preferred_element_type=WIDE)
        d_mixed = d_mixed.astype(LOW).astype(WIDE)
        parts = attend_back(hold[0, rows, :], hold[1, rows, :], hold[2, rows, :], d_mixed)
        for j in range(3):
            hold[j, rows, :] = parts[j]
    d_attn_ref[...] = total[...].astype(LOW)
    for j in range(3):
        d_triple_ref[j] = hold[j].astype(LOW)
    sums_ref[...] = jnp.concatenate(sums, axis=0)


def home(order, own_rows, share, me, blocks, marks, hot, route, router, res, cot, gain, proj, triple):
    _, count, cols = triple.shape
    width = res.shape[1]
    kernel = functools.partial(home_kernel, order, own_rows, share)
    whole = pl.BlockSpec(memory_space=pltpu.VMEM)
    operands = (*blocks, *marks, hot, route, router, res, cot, gain[None], proj, triple)
    return pl.pallas_call(
        kernel,
        out_shape=(
            jax.ShapeDtypeStruct((count, width), WIDE),
            jax.ShapeDtypeStruct((count, width), LOW),
            jax.ShapeDtypeStruct(triple.shape, LOW),
            jax.ShapeDtypeStruct(route.shape, LOW),
            jax.ShapeDtypeStruct((3, width), WIDE),
        ),
        in_specs=[pl.BlockSpec(memory_space=pltpu.SMEM)] + [whole] * len(operands),
        out_specs=[whole] * 5,
        scratch_shapes=[
            pltpu.VMEM((3, count, cols), WIDE),
            pltpu.VMEM((count, width), WIDE),
            pltpu.VMEM((len(order) * own_rows, width), LOW),
            pltpu.VMEM((2 * route.shape[0], len(order) * own_rows), LOW),
        ],
        compiler_params=pltpu.CompilerParams(vmem_limit_bytes=56 * 2**20),
        name="home",
    )(me.astype(jnp.int32).reshape(1), *operands)


def expert_kernel(share, first, me_ref, *refs):
    own_ref, peer_ref, cot_own_ref, cot_peer_ref, router_ref, b_in_ref, b_out_ref = refs[:7]
    pieces, refs = (refs[7:9], refs[9:]) if first else (refs[7:11], refs[11:])
    added, refs = ((), refs) if first else (refs[:2], refs[2:])
    mine_ref, peers_ref, hidden_ref, d_pre_ref, sums_ref = refs[:5]
    rows, cots = refs[6:8] if first else refs[5:7]
    w_in, w_out = pieces if first else refs[7:]
    half = pl.program_id(0)

    @pl.when(half == 0)
    def _():
        rows[...] = own_ref[...]
        cots[...] = cot_own_ref[...]
        if not first:
            for full, top, low in ((w_in, *pieces[:2]), (w_out, *pieces[2:])):
                full[: top.shape[0]] = top[...]
                full[top.shape[0] :] = low[...]
        sums_ref[...] = jnp.zeros_like(sums_ref)

    @pl.when(half == 1)
    def _():
        rows[...] = peer_ref[...]
        cots[...] = cot_peer_ref[...]

    given = rows[...]
    logits = jnp.dot(given, router_ref[...], preferred_element_type=WIDE)
    powers = jnp.exp(logits - jnp.max(logits, axis=1, keepdims=True))
    mine = lax.broadcasted_iota(jnp.int32, powers.shape, 1) == me_ref[0]
    gate = jnp.sum(jnp.where(mine, powers, 0.0), axis=1, keepdims=True)
    gate = gate / jnp.sum(powers, axis=1, keepdims=True)
    d_wide = (gate * cots[...].astype(WIDE)).astype(LOW)
    if first:
        refs[5][...] = d_wide
    pre = jnp.dot(given, w_in[...], preferred_element_type=WIDE) + b_in_ref[...]
    below = 0.5 * (1.0 + lax.erf(pre * ROOT_HALF))
    hidden = (pre * below).astype(LOW)
    hidden_ref[...] = hidden
    slope = below + pre * (DENSITY * jnp.exp(-0.5 * pre * pre))
    d_hidden = lax.dot_general(d_wide, w_out[...], dims(1, 1), preferred_element_type=WIDE)
    d_pre = (d_hidden * slope).astype(LOW)
    d_pre_ref[...] = d_pre
    out = jnp.dot(hidden, w_out[...], preferred_element_type=WIDE)
    back = lax.dot_general(d_pre, w_in[...], dims(1, 1), preferred_element_type=WIDE)
    sums_ref[0:1] += jnp.sum(d_pre.astype(WIDE), axis=0, keepdims=True)
    d_sum = jnp.sum(d_wide.astype(WIDE), axis=0, keepdims=True)
    blocks = (out.shape[0] // share, share, out.shape[1])

    @pl.when(half == 0)
    def _():
        full = (out if first else out + b_out_ref[...]).reshape(blocks)
        pair = jnp.concatenate([full, back.reshape(blocks)], axis=1)
        mine_ref[...] = (pair if first else pair + added[0][...].astype(WIDE)).astype(LOW)
        sums_ref[1:2] = d_sum

    @pl.when(half == 1)
    def _():
        pair = jnp.concatenate([out.reshape(blocks), back.reshape(blocks)], axis=1)
        peers_ref[...] = (pair if first else pair + added[1][...].astype(WIDE)).astype(LOW)
        sums_ref[2:3] = d_sum


def expert_work(share, me, rows, cots, router, b_in, b_out, w_in, w_out, added):
    count, width = rows[0].shape
    units = b_in.shape[1]
    first = not added
    operands = (*rows, *cots, router, b_in, b_out, *w_in, *w_out, *added)
    whole = [pl.BlockSpec(x.shape, lambda i, n=x.ndim: (0,) * n) for x in operands]
    moved = (count // share, 2 * share, width)
    each = lambda i: (i, 0)
    full = [] if first else [pltpu.VMEM((width, units), LOW), pltpu.VMEM((units, width), LOW)]
    return pl.pallas_call(
        functools.partial(expert_kernel, share, first),
        grid=(2,),
        out_shape=(
            jax.ShapeDtypeStruct(moved, LOW),
            jax.ShapeDtypeStruct(moved, LOW),
            jax.ShapeDtypeStruct((2 * count, units), LOW),
            jax.ShapeDtypeStruct((2 * count, units), LOW),
            jax.ShapeDtypeStruct((3, width), WIDE),
            jax.ShapeDtypeStruct((2 * count, width), LOW),
        )[: 6 if first else 5],
        in_specs=[pl.BlockSpec(memory_space=pltpu.SMEM)] + whole,
        out_specs=(
            pl.BlockSpec(moved, lambda i: (0, 0, 0)),
            pl.BlockSpec(moved, lambda i: (0, 0, 0)),
            pl.BlockSpec((count, units), each),
            pl.BlockSpec((count, units), each),
            pl.BlockSpec((3, width), lambda i: (0, 0)),
            pl.BlockSpec((count, width), each),
        )[: 6 if first else 5],
        scratch_shapes=[pltpu.VMEM((count, width), LOW)] * 2 + full,
        compiler_params=pltpu.CompilerParams(
            vmem_limit_bytes=52 * 2**20, dimension_semantics=("arbitrary",)
        ),
        name="expert_near" if first else "expert_far",
    )(me.astype(jnp.int32).reshape(1), *operands)


def on_device(
    tokens,
    ln1_gain,
    ln1_bias,
    w_qkv,
    b_qv,
    w_proj,
    b_proj,
    ln2_gain,
    ln2_bias,
    w_router,
    w_in,
    b_in,
    w_out,
    b_out,
    expert_ids,
    keep_mask,
    cotangent,
):
    tok_count, width = tokens.shape
    experts = w_router.shape[1]
    capacity = max(2, (2 * tok_count + experts - 1) // experts * 5 // 4)
    ranks = lax.axis_size("tensor")
    me_t, me_e = lax.axis_index("tensor"), lax.axis_index("expert")
    share = -(-capacity // (8 * ranks)) * 8
    local_cols = w_qkv.shape[2]
    order = tensor_order()

    far = ranks // 2
    cut = width // 2
    w_in_top, w_out_low = swap(w_in[0, :cut], far), swap(w_out[0, cut:], far)
    proj_all = placed_blocks(gather_list(w_proj), 0)

    ids = expert_ids.T
    kept = keep_mask.T > 0
    labels = jnp.arange(experts, dtype=jnp.int32)
    chosen = (ids[:, None, :] == labels[None, :, None])
    member = jnp.sum((chosen & kept[:, None, :]).astype(WIDE), axis=0)
    places = jnp.arange(tok_count, dtype=jnp.int32)
    earlier = (places[:, None] < places[None, :]).astype(LOW)
    before = dot_wide("et,ts->es", member.astype(LOW), earlier)
    slot = jnp.sum(jnp.where(chosen, before[None], 0.0), axis=1).astype(jnp.int32)
    holder = slot // share
    inner = ids * share + slot % share
    own_rows = experts * share
    own_place = jnp.where(kept & (holder == me_t), inner, -1)
    row_labels = jnp.arange(own_rows, dtype=jnp.int32)[:, None]
    own_hot = ((row_labels == own_place[0:1]) | (row_labels == own_place[1:2])).astype(LOW)
    all_place = jnp.where(kept, holder * own_rows + inner, -1).T
    all_labels = jnp.arange(ranks * own_rows, dtype=jnp.int32)[None, :]
    all_hot = ((all_labels == all_place[:, 0:1]) | (all_labels == all_place[:, 1:2])).astype(LOW)

    inputs = tokens.astype(WIDE)
    unit_one, scale_one = norm_parts(inputs)
    cot_rows = dot_wide("rt,td->rd", own_hot, cotangent.astype(LOW)).astype(LOW)
    own_tokens, cot_rows = together(tokens, cot_rows)
    cot_here = exchange(cot_rows)
    normed_low, triple, mixed_low = attend(own_tokens, ln1_gain, ln1_bias, w_qkv, b_qv)
    mixed_low, w_in_top = together(mixed_low, w_in_top)
    mixed_far = swap(mixed_low, far)
    mixed_far, w_in_rest = together(mixed_far, w_in[0, cut:])
    w_in_cuts = [w_in_top, swap(w_in_rest, far)]
    w_out_top = swap(w_out[0, :cut], far)
    mixed_all = placed_blocks(gather_list(mixed_low, mixed_far), 0)
    residual = inputs + (dot_wide("ct,cd->td", mixed_all, proj_all) + b_proj)
    unit_two, scale_two = norm_parts(residual)
    routed_low = (unit_two * ln2_gain + ln2_bias).astype(LOW)

    sent_rows = dot_wide("rt,td->rd", own_hot, routed_low).astype(LOW)
    sent_rows, cot_here, w_in_cuts[1] = together(sent_rows, cot_here, w_in_cuts[1])
    rows_here = exchange(sent_rows)
    rows_here, w_out_top = together(rows_here, w_out_top)
    rows_peer, b_in_far = swap(rows_here, 1), swap(b_in, far)
    rows_all = jnp.concatenate([rows_here, rows_peer], axis=0)
    shared = (share, me_e, (rows_here, rows_peer), (cot_here, swap(cot_here, 1)), w_router)
    far_out = (w_out_top, w_out_low)
    *added, near_hidden, near_pre, near_sums, d_rows = expert_work(
        *shared, b_in, b_out, (w_in[0],), (w_out[0],), ()
    )
    mine, peers, far_hidden, far_pre, far_sums = expert_work(
        *shared, b_in_far, b_out, w_in_cuts, far_out, added
    )
    hidden, d_pre = (near_hidden, far_hidden), (near_pre, far_pre)
    moved = exchange((mine.astype(WIDE) + swap(peers, 1).astype(WIDE)).astype(LOW))

    far_out = dot_wide("rf,rd->fd", hidden[1], d_rows).astype(LOW)
    far_in = dot_wide("rd,rf->df", rows_all, d_pre[1]).astype(LOW)
    out_arrived = swap(far_out, far)
    near_out = dot_wide("rf,rd->fd", hidden[0], d_rows)
    near_in = dot_wide("rd,rf->df", rows_all, d_pre[0])
    d_sum = near_sums[1] + near_sums[2]
    other_sums = swap(jnp.stack([far_sums[0], d_sum]), far)

    route = jax.nn.softmax(dot_wide("de,td->et", w_router, routed_low), axis=0)
    hot_blocks = own_hot.reshape(experts, share, tok_count).astype(WIDE)
    slot_gate = jnp.sum(hot_blocks * route[:, None, :], axis=2).reshape(own_rows, 1)
    moved, out_arrived, far_in = together(moved, out_arrived, far_in)
    grad_w_out = near_out + out_arrived.astype(WIDE)
    out_home = moved[:, :share].reshape(own_rows, width)
    back_home = moved[:, share:].reshape(own_rows, width)
    slot_grad = jnp.sum(cot_rows.astype(WIDE) * out_home.astype(WIDE), axis=1)
    marks = jnp.concatenate(halves(slot_grad.reshape(experts, share)), axis=0)
    marks = jnp.pad(marks, ((0, 0), (0, -share % 128))).astype(LOW)
    back_far, marks_far = together(swap(back_home, far), swap(marks, far))
    back_blocks, marks = gather_list(back_home, back_far), gather_list(marks, marks_far)
    gated = (slot_gate * out_home.astype(WIDE)).astype(LOW)
    back_blocks[1], gated, far_in = together(back_blocks[1], gated, far_in)
    mixture_part = dot_wide("rt,rd->td", own_hot, gated).astype(LOW)
    in_arrived = swap(far_in, far)
    d_residual, d_attn, d_triple, d_logits, sums = home(
        order,
        own_rows,
        share,
        me_t,
        back_blocks,
        marks,
        all_hot,
        route,
        w_router.T,
        residual,
        cotangent,
        ln2_gain,
        w_proj,
        triple,
    )
    grad_router = dot_wide("et,td->ed", d_logits, routed_low)
    grad_w_proj = dot_wide("ct,td->cd", mixed_low, d_attn)

    grad_w_qkv = dot_wide("jtc,td->jcd", d_triple, normed_low)
    grad_b_qv = jnp.stack(
        [jnp.sum(d_triple[0].astype(WIDE), axis=0), jnp.sum(d_triple[2].astype(WIDE), axis=0)]
    )
    d_normed_part = dot_wide("jtc,jdc->td", d_triple, w_qkv)
    grad_ln1_gain = jnp.sum(d_normed_part * unit_one, axis=0)
    grad_ln1_bias = jnp.sum(d_normed_part, axis=0)

    groups = lax.axis_size("expert")
    pair = jnp.pad(grad_b_qv.reshape(1, -1), ((0, 0), (0, width - 2 * local_cols)))
    small = jnp.stack([grad_ln1_gain, grad_ln1_bias])
    small = jnp.concatenate([small, sums, pair, grad_router], axis=0)
    count = small.shape[0]
    each = -(-count // groups)
    small = jnp.pad(small, ((0, groups * each - count), (0, 0))).reshape(groups, each, width)
    high, rest = halves(small)
    parts = grad_w_qkv.reshape(groups, -1, width)
    body = parts.shape[1]
    proj_parts = grad_w_proj.reshape(groups, -1, width)
    parts = jnp.concatenate([parts, proj_parts, high, rest], axis=1)
    proj_rows = proj_parts.shape[1]
    parts = jnp.pad(parts, ((0, 0), (0, -parts.shape[1] % 8), (0, 0)))
    parts, in_arrived, other_sums = together(parts, in_arrived, other_sums)
    grad_b_in = near_sums[0] + other_sums[0]
    grad_b_out = d_sum + other_sums[1]
    grad_w_in = near_in + in_arrived.astype(WIDE)

    rows_each = -(-tok_count // (16 * ranks)) * 16
    fill = ranks * rows_each - tok_count

    def rows_of(value, index):
        padded = jnp.pad(value, ((0, fill), (0, 0)))
        return lax.dynamic_slice_in_dim(padded, index * rows_each, rows_each, 0)

    both = jnp.concatenate([d_normed_part.astype(LOW), mixture_part], axis=1)
    shares = jnp.stack([rows_of(both, me_t ^ o) for o in order])
    shares = (shares[:2].astype(WIDE) + swap(shares[2:], 1).astype(WIDE)).astype(LOW)
    both = shares[0].astype(WIDE) + swap(shares[1], far).astype(WIDE)
    back = norm_back(
        rows_of(unit_one, me_t), rows_of(scale_one, me_t), ln1_gain, both[:, :width]
    )
    both = jnp.concatenate([back, both[:, width:]], axis=1).astype(LOW)

    def beside(done):
        pair, _ = together(both, done)
        pair = jnp.stack([pair, swap(pair, far)])
        pair = jnp.concatenate([pair, swap(pair, 1)], axis=0)
        full = jnp.zeros((ranks * rows_each, 2 * width), LOW)
        for place, o in enumerate(order):
            full = lax.dynamic_update_slice_in_dim(full, pair[place], (me_t ^ o) * rows_each, 0)
        full = full[:tok_count].astype(WIDE)
        return residual + full[:, width:], d_residual + full[:, :width]

    proj_sum, qkv_sum, small, (layer_out, grad_tokens) = expert_sum(
        parts, body, proj_rows, each, beside
    )
    proj_sum = proj_sum.reshape(local_cols, width)
    qkv_sum = jnp.swapaxes(qkv_sum.reshape(3, local_cols, width), 1, 2)
    small = small.reshape(groups * each, width)
    norm_sum = [small[:2]] + [swap(small[:2], step) for step in range(1, ranks)]
    norm_sum = (norm_sum[0] + norm_sum[1]) + sum(norm_sum[2:])
    return (
        layer_out,
        grad_tokens,
        norm_sum[0],
        norm_sum[1],
        qkv_sum,
        small[5, : 2 * local_cols].reshape(2, local_cols),
        proj_sum,
        small[4],
        small[2],
        small[3],
        small[6 : 6 + experts].T,
        grad_w_in[None],
        grad_b_in[None],
        grad_w_out[None],
        grad_b_out[None],
    )


def solution(mesh):
    placed = (
        P("expert", None),
        P(),
        P(),
        P(None, None, "tensor"),
        P(None, "tensor"),
        P("tensor", None),
        P(),
        P(),
        P(),
        P(),
        P("expert", None, "tensor"),
        P("expert", "tensor"),
        P("expert", "tensor", None),
        P("expert", None),
        P("expert", None),
        P("expert", None),
        P("expert", None),
    )
    return jax.shard_map(
        on_device,
        mesh=mesh,
        in_specs=placed,
        out_specs=(
            P("expert", None),
            P("expert", None),
            P(),
            P(),
            P(None, None, "tensor"),
            P(None, "tensor"),
            P("tensor", None),
            P(),
            P(),
            P(),
            P(),
            P("expert", None, "tensor"),
            P("expert", "tensor"),
            P("expert", "tensor", None),
            P("expert", None),
        ),
        check_vma=False,
    )
```
